32 devices in a mesh: dp: 4 (over y, core), ctx: 8 (over z, x).
Axes of the slice: x: 2, y: 2, z: 4, core: 2. Of those that a mesh axis runs over, the one named last changes fastest.
Arguments:
- queries: bfloat16 [4096, 2048], P(('dp', 'ctx')), parts along dimension 0, may hold values from -9 to 9
- keys: bfloat16 [4096, 512], P(('dp', 'ctx')), parts along dimension 0, may hold values from -9 to 9
- values: bfloat16 [4096, 512], P(('dp', 'ctx')), parts along dimension 0, may hold values from -6 to 6
- grad_out: bfloat16 [4096, 2048], P(('dp', 'ctx')), parts along dimension 0, may hold values from -6 to 6
- positions: int32 [1024], P('dp'), parts along dimension 0, may hold values from 0 to 1023, as said below
Outputs:
- attended: bfloat16 [4096, 2048], P(('dp', 'ctx')), parts along dimension 0
- grad_queries: bfloat16 [4096, 2048], P(('dp', 'ctx')), parts along dimension 0
- grad_keys: bfloat16 [4096, 512], P(('dp', 'ctx')), parts along dimension 0
- grad_values: bfloat16 [4096, 512], P(('dp', 'ctx')), parts along dimension 0
The draws below stay inside these ranges and needn't reach their ends.
There are 4 independent parts, one for each index of `dp`. The reference program is written for one: setup_inputs(seed, part) draws one part's arguments, and reference() takes and returns one part's arrays. A program takes and returns all parts, laid end to end along the dimension named above; each array names one. Nothing has to cross between parts.
Inputs may be any that keep to these rules, and one draw needn't show every extreme that they name: 256 distinct token positions in increasing order; the 128 tokens of one index of ctx hold at most 32 of them, and one index holds exactly 32.
All inputs are finite; a program needn't handle non-finite values.
Results may differ from the reference program's by a relative error of at most 0.0075.
Values may be sent and summed in bfloat16 or wider, within the bound.
A program may use at most 192 MiB of HBM per device.

```python
import math
import jax
import jax.numpy as jnp
from jax import lax

HQ = 16
HK = 4
DH = 128
BLOCK = 64
GLOB = 256
CAP = 32
TOK_DEV = 128
SEQ = 1024


def global_positions(key):
    baseline_value = jax.random.fold_in(key, 11)
    heavy_random_key, boost_random_key, jitter_random_key, shift_random_key = jax.random.split(baseline_value, 4)
    shard_pieces = SEQ // TOK_DEV
    heavy = jax.random.randint(heavy_random_key, (), 0, shard_pieces)
    extra_boost = jax.random.randint(boost_random_key, (shard_pieces,), 0, 2)
    random_jitter = jax.random.randint(jitter_random_key, (shard_pieces, CAP), 0, 1 << 14)
    shard_ids = jnp.arange(shard_pieces)[:, None]
    score_logit = random_jitter + extra_boost[:, None] * (1 << 13)
    score_logit = jnp.where(shard_ids == heavy, 1 << 16, score_logit)
    distinct = score_logit * (shard_pieces * CAP) + jnp.arange(shard_pieces * CAP).reshape(shard_pieces, CAP)
    unused, chosen = lax.top_k(distinct.reshape(-1), GLOB)
    picked = jnp.zeros((shard_pieces * CAP,), jnp.int32).at[chosen].set(1)
    offsets = jax.vmap(lambda one_key: jnp.sort(jax.random.permutation(one_key, TOK_DEV)[:CAP]))(jax.random.split(shift_random_key, shard_pieces))
    spots = (shard_ids * TOK_DEV + offsets).reshape(-1)
    ranked = jnp.where(picked == 1, spots, spots + SEQ)
    return jnp.sort(ranked)[:GLOB].astype(jnp.int32)


def draw_positions(key, part):
    return global_positions(key)


def draw_queries(key, part):
    inner = jax.random.fold_in(key, 31)
    drawn = jnp.clip(1.5 * jax.random.normal(inner, (SEQ, HQ * DH), jnp.float32), -9.0, 9.0)
    return drawn.astype(jnp.bfloat16)


def draw_keys(key, part):
    inner = jax.random.fold_in(key, 37)
    drawn = jnp.clip(1.5 * jax.random.normal(inner, (SEQ, HK * DH), jnp.float32), -9.0, 9.0)
    return drawn.astype(jnp.bfloat16)


def shard_levels(stream_key, shape, cuts, low, top_value):
    def one(position, blocks):
        draws = jax.random.uniform(jax.random.fold_in(jax.random.fold_in(stream_key, 6), position), (blocks,), jnp.float32, low / len(cuts), top_value / len(cuts))
        return jnp.repeat(jnp.exp(draws), shape[position] // blocks).reshape((-1,) + (1,) * (len(shape) - position - 1))

    loudness = one(*cuts[0])
    for cut in cuts[1:]:
        loudness = loudness * one(*cut)
    return loudness


def gaussian(key, extent, width, reach, cuts=(), dtype=jnp.bfloat16):
    level = shard_levels(key, extent, cuts, -0.22, 0.18) if cuts else 1.0
    array = jax.random.normal(key, extent, jnp.float32) * width * level
    return jnp.minimum(jnp.maximum(array, -reach), reach).astype(dtype)


def setup_inputs(seed: int = 0, part: int = 0) -> dict:
    streams_of = jax.random.split(jax.random.key(seed), 6)
    part_splits = jax.random.split(jax.random.fold_in(streams_of[5], part), 6)
    queries = draw_queries(jax.random.fold_in(jax.random.fold_in(streams_of[5], part), 71), part)
    keys = draw_keys(jax.random.fold_in(jax.random.fold_in(streams_of[5], part), 71), part)
    values = gaussian(part_splits[2], (SEQ, HK * DH), 1.0, 6.0, ((0, 8),))
    grad_out = gaussian(part_splits[3], (SEQ, HQ * DH), 1.0, 6.0, ((0, 8),))
    positions = draw_positions(jax.random.fold_in(jax.random.fold_in(streams_of[5], part), 71), part)
    return {"queries": queries, "keys": keys, "values": values, "grad_out": grad_out, "positions": positions}


highest = lax.Precision.HIGHEST

def rounded(source):
    return lax.optimization_barrier(source.astype(jnp.bfloat16)).astype(jnp.float32)

def window_group(pieces, glob_keys, glob_values, score_scale):
    query_block, grad_block, key_window, value_window, key_usable, query_live = pieces
    near = jnp.einsum('bqard,bkad->barqk', query_block, key_window, precision=highest) * score_scale
    far = jnp.einsum('bqard,gad->barqg', query_block, glob_keys, precision=highest) * score_scale
    near = jnp.where(key_usable[:, None, None, None, :], near, -jnp.inf)
    row_top = jnp.maximum(lax.optimization_barrier(jnp.max(near, axis=-1)), lax.optimization_barrier(jnp.max(far, axis=-1)))
    near_weight = jnp.exp(near - row_top[..., None])
    far_weight = jnp.exp(far - row_top[..., None])
    total = lax.optimization_barrier(jnp.sum(near_weight, axis=-1)) + lax.optimization_barrier(jnp.sum(far_weight, axis=-1))
    mixed = jnp.einsum('barqk,bkad->bqard', rounded(near_weight), value_window, precision=highest)
    mixed = mixed + jnp.einsum('barqg,gad->bqard', rounded(far_weight), glob_values, precision=highest)
    attended = mixed / jnp.transpose(total, (0, 3, 1, 2))[..., None]
    delta = jnp.transpose(lax.optimization_barrier(jnp.sum(grad_block * attended, axis=-1)), (0, 2, 3, 1))
    live = query_live[:, None, None, :, None]
    near_prob = near_weight / total[..., None]
    far_prob = far_weight / total[..., None]
    near_dprob = jnp.einsum('bqard,bkad->barqk', grad_block, value_window, precision=highest)
    far_dprob = jnp.einsum('bqard,gad->barqg', grad_block, glob_values, precision=highest)
    near_dscore = rounded(near_prob * (near_dprob - delta[..., None]) * live)
    far_dscore = rounded(far_prob * (far_dprob - delta[..., None]) * live)
    near_round = rounded(near_prob * live)
    far_round = rounded(far_prob * live)
    grad_query = jnp.einsum('barqk,bkad->bqard', near_dscore, key_window, precision=highest)
    grad_query = score_scale * (grad_query + jnp.einsum('barqg,gad->bqard', far_dscore, glob_keys, precision=highest))
    grad_key_win = score_scale * jnp.einsum('barqk,bqard->bkad', near_dscore, query_block, precision=highest)
    grad_value_win = jnp.einsum('barqk,bqard->bkad', near_round, grad_block, precision=highest)
    grad_key_glob = score_scale * jnp.einsum('barqg,bqard->gad', far_dscore, query_block, precision=highest)
    grad_value_glob = jnp.einsum('barqg,bqard->gad', far_round, grad_block, precision=highest)
    return (attended, grad_query, grad_key_win, grad_value_win, grad_key_glob, grad_value_glob)

def global_head(pieces, score_scale):
    query_head, grad_head, key_head, value_head = pieces
    score_logit = jnp.einsum('grd,ud->gru', query_head, key_head, precision=highest) * score_scale
    row_top = lax.optimization_barrier(jnp.max(score_logit, axis=-1))
    weight = jnp.exp(score_logit - row_top[..., None])
    total = lax.optimization_barrier(jnp.sum(weight, axis=-1))
    attended = jnp.einsum('gru,ud->grd', weight, value_head, precision=highest) / total[..., None]
    delta = lax.optimization_barrier(jnp.sum(grad_head * attended, axis=-1))
    prob = weight / total[..., None]
    dprob = jnp.einsum('grd,ud->gru', grad_head, value_head, precision=highest)
    dscore = rounded(prob * (dprob - delta[..., None]))
    prob_round = rounded(prob)
    grad_query = score_scale * jnp.einsum('gru,ud->grd', dscore, key_head, precision=highest)
    grad_key = score_scale * jnp.einsum('gru,grd->ud', dscore, query_head, precision=highest)
    grad_value = jnp.einsum('gru,grd->ud', prob_round, grad_head, precision=highest)
    return (attended, grad_query, grad_key, grad_value)

def spread_window(parts):
    empty_block = jnp.zeros((1,) + parts.shape[2:], jnp.float32)
    spread = jnp.concatenate([parts[:, 0], empty_block, empty_block], axis=0)
    spread = spread + jnp.concatenate([empty_block, parts[:, 1], empty_block], axis=0)
    spread = spread + jnp.concatenate([empty_block, empty_block, parts[:, 2]], axis=0)
    return spread[1:-1].reshape(SEQ, HK, DH)

def reference(queries, keys, values, grad_out, positions):
    q_per_kv = HQ // HK
    score_scale = 1.0 / math.sqrt(DH)
    blocks = SEQ // BLOCK
    query_all = queries.astype(jnp.float32).reshape(SEQ, HK, q_per_kv, DH)
    grad_all = grad_out.astype(jnp.float32).reshape(SEQ, HK, q_per_kv, DH)
    key_all = keys.astype(jnp.float32).reshape(SEQ, HK, DH)
    value_all = values.astype(jnp.float32).reshape(SEQ, HK, DH)
    is_global = jnp.zeros((SEQ,), jnp.int32).at[positions].set(1)
    padding = jnp.zeros((BLOCK, HK, DH), jnp.float32)
    key_ext = jnp.concatenate([padding, key_all, padding], axis=0).reshape(blocks + 2, BLOCK, HK, DH)
    value_ext = jnp.concatenate([padding, value_all, padding], axis=0).reshape(blocks + 2, BLOCK, HK, DH)
    key_window = jnp.concatenate([key_ext[:-2], key_ext[1:-1], key_ext[2:]], axis=1)
    value_window = jnp.concatenate([value_ext[:-2], value_ext[1:-1], value_ext[2:]], axis=1)
    border = jnp.ones((BLOCK,), jnp.int32)
    ext_usable = (jnp.concatenate([border, is_global, border]) == 0).reshape(blocks + 2, BLOCK)
    key_usable = jnp.concatenate([ext_usable[:-2], ext_usable[1:-1], ext_usable[2:]], axis=1)
    query_live = (1 - is_global).astype(jnp.float32).reshape(blocks, BLOCK)
    glob_keys = key_all[positions]
    glob_values = value_all[positions]
    per_step = 8
    step_count = blocks // per_step

    def regroup(source):
        return source.reshape((step_count, per_step) + source.shape[1:])
    stacked = (regroup(query_all.reshape(blocks, BLOCK, HK, q_per_kv, DH)), regroup(grad_all.reshape(blocks, BLOCK, HK, q_per_kv, DH)), regroup(key_window), regroup(value_window), regroup(key_usable), regroup(query_live))
    results = lax.map(lambda pieces: window_group(pieces, glob_keys, glob_values, score_scale), stacked)
    attended_loc = results[0].reshape(SEQ, HK, q_per_kv, DH)
    grad_query_loc = results[1].reshape(SEQ, HK, q_per_kv, DH)
    key_parts = results[2].reshape(blocks, 3, BLOCK, HK, DH)
    value_parts = results[3].reshape(blocks, 3, BLOCK, HK, DH)
    glob_key_grad = lax.optimization_barrier(jnp.sum(results[4], axis=0))
    glob_value_grad = lax.optimization_barrier(jnp.sum(results[5], axis=0))
    head_inputs = (jnp.transpose(query_all[positions], (1, 0, 2, 3)), jnp.transpose(grad_all[positions], (1, 0, 2, 3)), jnp.transpose(key_all, (1, 0, 2)), jnp.transpose(value_all, (1, 0, 2)))
    head_out = lax.map(lambda pieces: global_head(pieces, score_scale), head_inputs)
    attended = attended_loc.at[positions].set(jnp.transpose(head_out[0], (1, 0, 2, 3)))
    grad_query = grad_query_loc.at[positions].add(jnp.transpose(head_out[1], (1, 0, 2, 3)))
    grad_key = spread_window(key_parts).at[positions].add(glob_key_grad) + jnp.transpose(head_out[2], (1, 0, 2))
    grad_value = spread_window(value_parts).at[positions].add(glob_value_grad) + jnp.transpose(head_out[3], (1, 0, 2))
    return (attended.reshape(SEQ, HQ * DH).astype(jnp.bfloat16), grad_query.reshape(SEQ, HQ * DH).astype(jnp.bfloat16), grad_key.reshape(SEQ, HK * DH).astype(jnp.bfloat16), grad_value.reshape(SEQ, HK * DH).astype(jnp.bfloat16))
```

```python
import functools
import math

import jax
import jax.numpy as jnp
from jax import lax
from jax.experimental import pallas as pl
from jax.experimental.pallas import tpu as pltpu
from jax.sharding import PartitionSpec as P

HQ = 16
HK = 4
DH = 128
BLOCK = 64
CAP = 32


highest = lax.Precision.HIGHEST


def with_halo(array, sides, width):
    for axis, dim in sides:
        size, length = (lax.axis_size(axis), array.shape[dim])
        up = [(i, (i + 1) % size) for i in range(size - 1)]
        down = [(j, i) for i, j in up]
        last = lax.slice_in_dim(array, length - width, length, axis=dim)
        first = lax.slice_in_dim(array, 0, width, axis=dim)
        before = lax.ppermute(last, axis, up)
        after = lax.ppermute(first, axis, down)
        array = jnp.concatenate([before, array, after], axis=dim)
    return array


def combined_all(part, axis, combine):
    gathered = jax.tree.map(lambda a: lax.all_gather(a, axis), part)

    def take(source):
        return jax.tree.map(lambda a: lax.dynamic_index_in_dim(a, source, 0, False), gathered)

    return lax.fori_loop(
        1, lax.axis_size(axis), lambda source, state: combine(state, take(source)), take(0)
    )


def window_group(pieces, glob_keys, glob_values, score_scale):
    query_block, grad_block, key_window, value_window, key_usable, query_live = pieces
    near = (
        jnp.einsum("bqard,bkad->barqk", query_block, key_window, preferred_element_type=jnp.float32)
        * score_scale
    )
    far = (
        jnp.einsum("bqard,gad->barqg", query_block, glob_keys, preferred_element_type=jnp.float32)
        * score_scale
    )
    near = jnp.where(key_usable[:, None, None, None, :], near, -jnp.inf)
    row_top = jnp.maximum(jnp.max(near, axis=-1), jnp.max(far, axis=-1))
    near_weight = jnp.exp(near - row_top[..., None])
    far_weight = jnp.exp(far - row_top[..., None])
    total = jnp.sum(near_weight, axis=-1) + jnp.sum(far_weight, axis=-1)
    mixed = jnp.einsum(
        "barqk,bkad->bqard",
        near_weight.astype(jnp.bfloat16),
        value_window,
        preferred_element_type=jnp.float32,
    )
    mixed = mixed + jnp.einsum(
        "barqg,gad->bqard",
        far_weight.astype(jnp.bfloat16),
        glob_values,
        preferred_element_type=jnp.float32,
    )
    attended = mixed / jnp.transpose(total, (0, 3, 1, 2))[..., None]
    delta = jnp.transpose(jnp.sum(grad_block * attended, axis=-1), (0, 2, 3, 1))
    live = query_live[:, None, None, :, None]
    near_prob = near_weight / total[..., None]
    far_prob = far_weight / total[..., None]
    near_dprob = jnp.einsum(
        "bqard,bkad->barqk", grad_block, value_window, preferred_element_type=jnp.float32
    )
    far_dprob = jnp.einsum(
        "bqard,gad->barqg", grad_block, glob_values, preferred_element_type=jnp.float32
    )
    near_dscore = (near_prob * (near_dprob - delta[..., None]) * live).astype(jnp.bfloat16)
    far_dscore = (far_prob * (far_dprob - delta[..., None]) * live).astype(jnp.bfloat16)
    near_round = (near_prob * live).astype(jnp.bfloat16)
    far_round = (far_prob * live).astype(jnp.bfloat16)
    grad_query = jnp.einsum(
        "barqk,bkad->bqard", near_dscore, key_window, preferred_element_type=jnp.float32
    )
    grad_query = score_scale * (
        grad_query
        + jnp.einsum("barqg,gad->bqard", far_dscore, glob_keys, preferred_element_type=jnp.float32)
    )
    grad_key_win = score_scale * jnp.einsum(
        "barqk,bqard->bkad", near_dscore, query_block, preferred_element_type=jnp.float32
    )
    grad_value_win = jnp.einsum(
        "barqk,bqard->bkad", near_round, grad_block, preferred_element_type=jnp.float32
    )
    grad_key_glob = score_scale * jnp.einsum(
        "barqg,bqard->gad", far_dscore, query_block, preferred_element_type=jnp.float32
    )
    grad_value_glob = jnp.einsum(
        "barqg,bqard->gad", far_round, grad_block, preferred_element_type=jnp.float32
    )
    return (attended, grad_query, grad_key_win, grad_value_win, grad_key_glob, grad_value_glob)


def combine_softmax(left_part, right_part):
    left_top, left_total, left_summed = left_part
    right_top, right_total, right_summed = right_part
    joint_top = jnp.maximum(left_top, right_top)
    left_factor = jnp.exp(left_top - joint_top)
    right_factor = jnp.exp(right_top - joint_top)
    return (
        joint_top,
        left_total * left_factor + right_total * right_factor,
        left_summed * left_factor[..., None] + right_summed * right_factor[..., None],
    )


def local(queries, keys, values, grad_out, positions):
    tok_rows = queries.shape[0]
    query_width = queries.shape[1]
    key_width = keys.shape[1]
    q_per_kv = HQ // HK
    ctx_count = lax.axis_size("ctx")
    seq_total = tok_rows * ctx_count
    first_row = lax.axis_index("ctx") * tok_rows
    score_scale = 1.0 / math.sqrt(DH)
    glob_count = positions.shape[0]
    local_row = positions - first_row
    is_mine = (local_row >= 0) & (local_row < tok_rows)
    safe_row = jnp.clip(local_row, 0, tok_rows - 1)
    before = jnp.sum((positions < first_row).astype(jnp.int32))
    held_count = jnp.sum(is_mine.astype(jnp.int32))
    slot_index = jnp.arange(CAP)
    slot_ok = slot_index < held_count
    slot_row = jnp.clip(
        positions[jnp.clip(before + slot_index, 0, glob_count - 1)] - first_row, 0, tok_rows - 1
    )
    owner_index = positions // tok_rows
    owner_start = jnp.sum((owner_index[None, :] < owner_index[:, None]).astype(jnp.int32), axis=1)
    slot_of = owner_index * CAP + jnp.arange(glob_count) - owner_start
    packed = jnp.concatenate(
        [queries[slot_row], keys[slot_row], values[slot_row], grad_out[slot_row]], axis=1
    )
    packed = jnp.where(slot_ok[:, None], packed, jnp.zeros_like(packed))
    everyone = lax.all_gather(packed, "ctx", axis=0, tiled=True)
    compact = everyone[slot_of]
    glob_query = compact[:, :query_width].reshape(glob_count, HK, q_per_kv, DH)
    glob_keys = compact[:, query_width : query_width + key_width].reshape(glob_count, HK, DH)
    glob_values = compact[:, query_width + key_width : query_width + 2 * key_width].reshape(
        glob_count, HK, DH
    )
    glob_grad = compact[:, query_width + 2 * key_width :].reshape(glob_count, HK, q_per_kv, DH)
    paired = jnp.concatenate([keys, values], axis=1)
    extended = with_halo(paired, (("ctx", 0),), BLOCK)
    blocks = tok_rows // BLOCK
    ext_blocks = extended.reshape(blocks + 2, BLOCK, 2 * key_width)
    window = jnp.concatenate([ext_blocks[:-2], ext_blocks[1:-1], ext_blocks[2:]], axis=1)
    key_window = window[:, :, :key_width].reshape(blocks, 3 * BLOCK, HK, DH)
    value_window = window[:, :, key_width:].reshape(blocks, 3 * BLOCK, HK, DH)
    ext_position = first_row - BLOCK + jnp.arange(tok_rows + 2 * BLOCK)
    ext_global = jnp.any(ext_position[:, None] == positions[None, :], axis=1)
    ext_usable = (
        (ext_position >= 0) & (ext_position < seq_total) & jnp.logical_not(ext_global)
    ).reshape(blocks + 2, BLOCK)
    key_usable = jnp.concatenate([ext_usable[:-2], ext_usable[1:-1], ext_usable[2:]], axis=1)
    query_live = (
        jnp.logical_not(ext_global[BLOCK : BLOCK + tok_rows])
        .astype(jnp.float32)
        .reshape(blocks, BLOCK)
    )
    per_step = min(8, blocks)
    step_count = blocks // per_step

    def regroup(source):
        return source.reshape((step_count, per_step) + source.shape[1:])

    stacked = (
        regroup(queries.reshape(blocks, BLOCK, HK, q_per_kv, DH)),
        regroup(grad_out.reshape(blocks, BLOCK, HK, q_per_kv, DH)),
        regroup(key_window),
        regroup(value_window),
        regroup(key_usable),
        regroup(query_live),
    )
    results = lax.map(
        lambda pieces: window_group(pieces, glob_keys, glob_values, score_scale), stacked
    )
    attended_loc = results[0].reshape(tok_rows, query_width)
    grad_query_loc = results[1].reshape(tok_rows, query_width)
    window_grads = jnp.concatenate(
        [
            results[2].reshape(blocks, 3, BLOCK, key_width),
            results[3].reshape(blocks, 3, BLOCK, key_width),
        ],
        axis=3,
    )
    glob_key_grad = jnp.sum(results[4], axis=0).reshape(glob_count, key_width)
    glob_value_grad = jnp.sum(results[5], axis=0).reshape(glob_count, key_width)
    key_here = keys.reshape(tok_rows, HK, DH)
    value_here = values.reshape(tok_rows, HK, DH)
    glob_score = (
        jnp.einsum("gard,uad->argu", glob_query, key_here, preferred_element_type=jnp.float32)
        * score_scale
    )
    top_here = jnp.max(glob_score, axis=-1)
    weight_here = jnp.exp(glob_score - top_here[..., None])
    total_here = jnp.sum(weight_here, axis=-1)
    summed_here = jnp.einsum(
        "argu,uad->argd", weight_here, value_here.astype(jnp.float32), precision=highest
    )
    glob_top, glob_total, glob_summed = combined_all(
        (top_here, total_here, summed_here), "ctx", combine_softmax
    )
    glob_attended = glob_summed / glob_total[..., None]
    glob_delta = jnp.sum(
        jnp.transpose(glob_grad, (1, 2, 0, 3)).astype(jnp.float32) * glob_attended, axis=-1
    )
    glob_prob = jnp.exp(glob_score - glob_top[..., None]) / glob_total[..., None]
    glob_dprob = jnp.einsum(
        "gard,uad->argu", glob_grad, value_here, preferred_element_type=jnp.float32
    )
    glob_dscore = (glob_prob * (glob_dprob - glob_delta[..., None])).astype(jnp.bfloat16)
    glob_round = glob_prob.astype(jnp.bfloat16)
    glob_query_grad = score_scale * jnp.einsum(
        "argu,uad->gard", glob_dscore, key_here, preferred_element_type=jnp.float32
    )
    key_grad_here = score_scale * jnp.einsum(
        "argu,gard->uad", glob_dscore, glob_query, preferred_element_type=jnp.float32
    )
    value_grad_here = jnp.einsum(
        "argu,gard->uad", glob_round, glob_grad, preferred_element_type=jnp.float32
    )
    empty_block = jnp.zeros((1, BLOCK, 2 * key_width), jnp.float32)
    spread = jnp.concatenate([window_grads[:, 0], empty_block, empty_block], axis=0)
    spread = spread + jnp.concatenate([empty_block, window_grads[:, 1], empty_block], axis=0)
    spread = spread + jnp.concatenate([empty_block, empty_block, window_grads[:, 2]], axis=0)
    rims = jnp.concatenate([spread[0], spread[-1]], axis=0)
    arrived = with_halo(rims, (("ctx", 0),), BLOCK)
    pair_grad = spread[1:-1].reshape(tok_rows, 2 * key_width)
    pair_grad = pair_grad.at[:BLOCK].add(arrived[:BLOCK])
    pair_grad = pair_grad.at[tok_rows - BLOCK :].add(arrived[3 * BLOCK :])
    pair_grad = pair_grad + jnp.concatenate(
        [key_grad_here.reshape(tok_rows, key_width), value_grad_here.reshape(tok_rows, key_width)],
        axis=1,
    )
    glob_grads = jnp.concatenate(
        [glob_query_grad.reshape(glob_count, query_width), glob_key_grad, glob_value_grad], axis=1
    )
    laid = (
        jnp.zeros((ctx_count * CAP, glob_grads.shape[1]), jnp.float32).at[slot_of].set(glob_grads)
    )
    returned = lax.psum_scatter(laid, "ctx", scatter_dimension=0, tiled=True)
    target = jnp.where(slot_ok, slot_row, tok_rows)
    grad_query_all = grad_query_loc.at[target].add(returned[:, :query_width], mode="drop")
    pair_grad = pair_grad.at[target].add(returned[:, query_width:], mode="drop")
    glob_rows_out = jnp.transpose(glob_attended, (2, 0, 1, 3)).reshape(glob_count, query_width)
    attended_all = attended_loc.at[jnp.where(is_mine, safe_row, tok_rows)].set(
        glob_rows_out, mode="drop"
    )
    return (
        attended_all.astype(jnp.bfloat16),
        grad_query_all.astype(jnp.bfloat16),
        pair_grad[:, :key_width].astype(jnp.bfloat16),
        pair_grad[:, key_width:].astype(jnp.bfloat16),
    )


MESH = pl.DeviceIdType.MESH
ROWS = 4
REP = HQ // HK
TOK = 128
FAR = -1e30


def dense_kernel(
    pos_row, pos_col, q_ref, k_ref, v_ref, g_ref,
    att_ref, gq_ref, gk_ref, gv_ref,
    kbuf, vbuf, qt, gt, qs, gs, sbuf, dbuf, pbuf, wbuf, top8, inv, delta,
    acc, xsend, xrecv, csend, crecv,
    ax_s, ax_r, au_s, au_r, ad_s, ad_r, rx_s, rx_r, rc_s, rc_r,
):
    c = lax.axis_index("ctx")
    z, x = c // 2, c % 2
    partner = c + 1 - 2 * x
    scale = 1.0 / math.sqrt(DH)
    own = (k_ref, v_ref)
    bufs = (kbuf, vbuf)
    wide = REP * TOK

    def rows(block):
        return pl.ds(pl.multiple_of(block * TOK, TOK), TOK)

    def head(j):
        return pl.ds(pl.multiple_of(j * DH, DH), DH)

    barrier = pltpu.get_barrier_semaphore()
    pl.semaphore_signal(barrier, inc=1, device_id={"ctx": partner}, device_id_type=MESH)

    @pl.when(z > 0)
    def _():
        pl.semaphore_signal(barrier, inc=1, device_id={"ctx": c - 2}, device_id_type=MESH)

    @pl.when(z < ROWS - 1)
    def _():
        pl.semaphore_signal(barrier, inc=1, device_id={"ctx": c + 2}, device_id_type=MESH)

    pl.semaphore_wait(
        barrier, 1 + (z > 0).astype(jnp.int32) + (z < ROWS - 1).astype(jnp.int32)
    )

    def remote(source, target, send, recv, device):
        return pltpu.make_async_remote_copy(
            src_ref=source, dst_ref=target, send_sem=send, recv_sem=recv,
            device_id={"ctx": device}, device_id_type=MESH,
        )

    def along(h, k, up, source=None):
        block = c - 2 * (k - 1) if up else c + 2 * (k - 1)
        here = bufs[h].at[rows(block)]
        send, recv = (au_s, au_r) if up else (ad_s, ad_r)
        return remote(
            here if source is None else source, here,
            send.at[h, k - 1], recv.at[h, k - 1], c + 2 if up else c - 2,
        )

    def along_in(h, k, up):
        block = c - 2 * k if up else c + 2 * k
        here = bufs[h].at[rows(block)]
        send, recv = (au_s, au_r) if up else (ad_s, ad_r)
        return remote(here, here, send.at[h, k - 1], recv.at[h, k - 1], partner)

    def across(h, zz, source=None):
        here = bufs[h].at[rows(2 * zz + x)]
        return remote(
            here if source is None else source, here, ax_s.at[h, zz], ax_r.at[h, zz], partner
        )

    def across_in(h, zz):
        here = bufs[h].at[rows(2 * zz + 1 - x)]
        return remote(here, here, ax_s.at[h, zz], ax_r.at[h, zz], partner)

    for h in (0, 1):
        across(h, z, own[h]).start()

        @pl.when(z < ROWS - 1)
        def _():
            along(h, 1, True, own[h]).start()

        @pl.when(z > 0)
        def _():
            along(h, 1, False, own[h]).start()

    kbuf[rows(c), :] = k_ref[...]
    vbuf[rows(c), :] = v_ref[...]

    def stack(j, carry):
        for r in range(REP):
            cols = pl.ds(pl.multiple_of((j * REP + r) * DH, DH), DH)
            part = q_ref[:, cols]
            qs[j, r * TOK : (r + 1) * TOK, :] = part
            qt[j, :, r * TOK : (r + 1) * TOK] = part.astype(jnp.float32).T.astype(jnp.bfloat16)
            part = g_ref[:, cols]
            gs[j, r * TOK : (r + 1) * TOK, :] = part
            gt[j, :, r * TOK : (r + 1) * TOK] = part.astype(jnp.float32).T.astype(jnp.bfloat16)
        return carry

    lax.fori_loop(0, HK, stack, 0)
    top8[...] = jnp.full(top8.shape, FAR, jnp.float32)

    glob_count = pos_row.shape[1]
    row_token = c * TOK + lax.broadcasted_iota(jnp.int32, (glob_count, TOK), 1)
    row_glob = jnp.max(
        jnp.where(pos_col[...] == row_token, 1.0, 0.0), axis=0, keepdims=True
    )

    def block_bias(block):
        col_token = block * TOK + lax.broadcasted_iota(jnp.int32, (TOK, glob_count), 0)
        col_glob = jnp.max(
            jnp.where(pos_row[...] == col_token, 1.0, 0.0), axis=1, keepdims=True
        )
        u_block = block * (TOK // BLOCK) + lax.broadcasted_iota(jnp.int32, (TOK, TOK), 0) // BLOCK
        t_block = c * (TOK // BLOCK) + lax.broadcasted_iota(jnp.int32, (TOK, TOK), 1) // BLOCK
        near = jnp.where(jnp.abs(u_block - t_block) <= 1, 1.0, 0.0)
        allowed = jnp.maximum(jnp.maximum(near, row_glob), col_glob)
        bias = jnp.where(allowed > 0.5, 0.0, FAR)
        return jnp.concatenate([bias] * REP, axis=1)

    def scores(block):
        bias = block_bias(block)
        at = rows(block)

        def one(j, carry):
            s = jnp.dot(kbuf[at, head(j)], qt[j], preferred_element_type=jnp.float32)
            s = s * scale + bias
            sbuf[j, at, :] = s
            top8[j] = jnp.maximum(top8[j], jnp.max(s.reshape(TOK // 8, 8, wide), axis=0))
            dbuf[j, at, :] = jnp.dot(
                vbuf[at, head(j)], gt[j], preferred_element_type=jnp.float32
            )
            return carry

        lax.fori_loop(0, HK, one, 0)

    scores(c)

    def gather_step(k, carry):
        @pl.when(z - k >= 0)
        def _():
            for h in (0, 1):
                along_in(h, k, True).wait_recv()

                @pl.when(z < ROWS - 1)
                def _():
                    along(h, k + 1, True).start()

                across(h, z - k).start()

        @pl.when(z + k < ROWS)
        def _():
            for h in (0, 1):
                along_in(h, k, False).wait_recv()

                @pl.when(z > 0)
                def _():
                    along(h, k + 1, False).start()

                across(h, z + k).start()

        @pl.when(z - k >= 0)
        def _():
            scores(c - 2 * k)

        @pl.when(z + k < ROWS)
        def _():
            scores(c + 2 * k)

        @pl.when(z - (k - 1) >= 0)
        def _():
            for h in (0, 1):
                across_in(h, z - (k - 1)).wait_recv()
            scores(2 * (z - (k - 1)) + 1 - x)

        @pl.when((z + (k - 1) < ROWS) & (k > 1))
        def _():
            for h in (0, 1):
                across_in(h, z + (k - 1)).wait_recv()
            scores(2 * (z + (k - 1)) + 1 - x)

        return carry

    lax.fori_loop(1, ROWS + 1, gather_step, 0)

    def stats(j, carry):
        top = jnp.max(top8[j], axis=0, keepdims=True)

        def part(b, sums):
            total8, mixed8 = sums
            at = rows(b)
            e = jnp.exp(sbuf[j, at, :] - top)
            sbuf[j, at, :] = e
            total8 = total8 + jnp.sum(e.reshape(TOK // 8, 8, wide), axis=0)
            e = e * dbuf[j, at, :]
            return total8, mixed8 + jnp.sum(e.reshape(TOK // 8, 8, wide), axis=0)

        zero = jnp.zeros((8, wide), jnp.float32)
        total8, mixed8 = lax.fori_loop(0, 2 * ROWS, part, (zero, zero))
        reciprocal = 1.0 / jnp.sum(total8, axis=0, keepdims=True)
        inv[j] = jnp.broadcast_to(reciprocal, (8, wide))
        delta[j] = jnp.broadcast_to(
            jnp.sum(mixed8, axis=0, keepdims=True) * reciprocal, (8, wide)
        )
        return carry

    lax.fori_loop(0, HK, stats, 0)

    def terms(block, out):
        at = rows(block)

        def one(j, carry):
            p = sbuf[j, at, :] * inv[j, 0:1, :]
            w = (p * (dbuf[j, at, :] - delta[j, 0:1, :])).astype(jnp.bfloat16)
            p = p.astype(jnp.bfloat16)
            pbuf[j, at, :] = p
            wbuf[j, at, :] = w
            dk = jnp.dot(w, qs[j], preferred_element_type=jnp.float32) * scale
            dv = jnp.dot(p, gs[j], preferred_element_type=jnp.float32)
            out[0, :, head(j)] = dk.astype(out.dtype)
            out[1, :, head(j)] = dv.astype(out.dtype)
            return carry

        lax.fori_loop(0, HK, one, 0)

    def pick(a, b, d, e):
        return jnp.where(z == 0, a, jnp.where(z == 1, b, jnp.where(z == 2, d, e)))

    order = (pick(3, 3, 0, 0), pick(2, 0, 3, 1), pick(1, 2, 1, 2), z)

    def cross(h, o):
        return remote(
            xsend.at[o, h], xrecv.at[o, h], rx_s.at[h, o], rx_r.at[h, o], partner
        )

    def phase(o):
        terms(2 * order[o] + 1 - x, xsend.at[o])
        for h in (0, 1):
            cross(h, o).start()
        terms(2 * order[o] + x, acc.at[o])

    def chain(h, o):
        down = order[o] < z
        to = jnp.where(down, z - 1, z + 1)
        slot = jnp.where((to == order[o]) & jnp.logical_not(down), ROWS, order[o])
        return remote(
            csend.at[o, h], crecv.at[slot, h], rc_s.at[h, o], rc_r.at[h, slot], 2 * to + x
        )

    def chain_in(h, slot):
        return remote(crecv.at[slot, h], crecv.at[slot, h], rc_s.at[h, 0], rc_r.at[h, slot], partner)

    def pass_on(o):
        down = order[o] < z
        fed = (down & (z < ROWS - 1)) | (jnp.logical_not(down) & (z > 0))
        for h in (0, 1):
            cross(h, o).wait_recv()
            acc[o, h] = acc[o, h] + xrecv[o, h].astype(jnp.float32)

            @pl.when(fed)
            def _():
                chain_in(h, order[o]).wait_recv()
                acc[o, h] = acc[o, h] + crecv[order[o], h].astype(jnp.float32)

            csend[o, h] = acc[o, h].astype(jnp.bfloat16)
            chain(h, o).start()

    phase(0)
    phase(1)
    phase(2)
    pass_on(0)
    phase(3)

    def outputs(j, carry):
        across_rows = (((0,), (0,)), ((), ()))
        mixed = lax.dot_general(
            vbuf[:, head(j)], pbuf[j], across_rows, preferred_element_type=jnp.float32
        )
        grad = scale * lax.dot_general(
            kbuf[:, head(j)], wbuf[j], across_rows, preferred_element_type=jnp.float32
        )
        for r in range(REP):
            cols = pl.ds(pl.multiple_of((j * REP + r) * DH, DH), DH)
            att_ref[:, cols] = mixed[:, r * TOK : (r + 1) * TOK].T.astype(jnp.bfloat16)
            gq_ref[:, cols] = grad[:, r * TOK : (r + 1) * TOK].T.astype(jnp.bfloat16)
        return carry

    lax.fori_loop(0, HK, outputs, 0)

    pass_on(1)
    pass_on(2)
    last = ROWS - 1
    for h, out in ((0, gk_ref), (1, gv_ref)):
        cross(h, last).wait_recv()
        acc[last, h] = acc[last, h] + xrecv[last, h].astype(jnp.float32)

        @pl.when(z < ROWS - 1)
        def _():
            chain_in(h, z).wait_recv()
            acc[last, h] = acc[last, h] + crecv[z, h].astype(jnp.float32)

        @pl.when(z > 0)
        def _():
            chain_in(h, ROWS).wait_recv()
            acc[last, h] = acc[last, h] + crecv[ROWS, h].astype(jnp.float32)

        out[...] = acc[last, h].astype(jnp.bfloat16)

    for h in (0, 1):
        for zz in range(ROWS):
            across(h, zz).wait_send()
            cross(h, zz).wait_send()
        for o in range(ROWS - 1):
            chain(h, o).wait_send()
        for k in range(1, ROWS):

            @pl.when((z - (k - 1) >= 0) & (z < ROWS - 1))
            def _():
                along(h, k, True).wait_send()

            @pl.when((z + (k - 1) < ROWS) & (z > 0))
            def _():
                along(h, k, False).wait_send()


def dense(queries, keys, values, grad_out, positions):
    tokens = TOK * 2 * ROWS
    key_width = HK * DH
    wide = REP * TOK
    bf16, f32 = jnp.bfloat16, jnp.float32
    vmem = pl.BlockSpec(memory_space=pltpu.VMEM)
    dma = pltpu.SemaphoreType.DMA
    return pl.pallas_call(
        dense_kernel,
        out_shape=[
            jax.ShapeDtypeStruct((TOK, HQ * DH), bf16),
            jax.ShapeDtypeStruct((TOK, HQ * DH), bf16),
            jax.ShapeDtypeStruct((TOK, key_width), bf16),
            jax.ShapeDtypeStruct((TOK, key_width), bf16),
        ],
        in_specs=[vmem] * 6,
        out_specs=[vmem] * 4,
        scratch_shapes=[
            pltpu.VMEM((tokens, key_width), bf16),
            pltpu.VMEM((tokens, key_width), bf16),
            pltpu.VMEM((HK, DH, wide), bf16),
            pltpu.VMEM((HK, DH, wide), bf16),
            pltpu.VMEM((HK, wide, DH), bf16),
            pltpu.VMEM((HK, wide, DH), bf16),
            pltpu.VMEM((HK, tokens, wide), f32),
            pltpu.VMEM((HK, tokens, wide), f32),
            pltpu.VMEM((HK, tokens, wide), bf16),
            pltpu.VMEM((HK, tokens, wide), bf16),
            pltpu.VMEM((HK, 8, wide), f32),
            pltpu.VMEM((HK, 8, wide), f32),
            pltpu.VMEM((HK, 8, wide), f32),
            pltpu.VMEM((ROWS, 2, TOK, key_width), f32),
            pltpu.VMEM((ROWS, 2, TOK, key_width), bf16),
            pltpu.VMEM((ROWS, 2, TOK, key_width), bf16),
            pltpu.VMEM((ROWS - 1, 2, TOK, key_width), bf16),
            pltpu.VMEM((ROWS + 1, 2, TOK, key_width), bf16),
            dma((2, ROWS)),
            dma((2, ROWS)),
            dma((2, ROWS - 1)),
            dma((2, ROWS - 1)),
            dma((2, ROWS - 1)),
            dma((2, ROWS - 1)),
            dma((2, ROWS)),
            dma((2, ROWS)),
            dma((2, ROWS - 1)),
            dma((2, ROWS + 1)),
        ],
        compiler_params=pltpu.CompilerParams(
            collective_id=0, has_side_effects=True, vmem_limit_bytes=56 * 1024 * 1024
        ),
    )(
        positions.reshape(1, -1), positions.reshape(-1, 1),
        queries, keys, values, grad_out,
    )


def choose(queries, keys, values, grad_out, positions):
    if lax.axis_size("ctx") == 2 * ROWS and queries.shape[0] == TOK:
        return tuple(dense(queries, keys, values, grad_out, positions))
    return local(queries, keys, values, grad_out, positions)


def solution(mesh):
    in_specs = (
        P(("dp", "ctx"), None),
        P(("dp", "ctx"), None),
        P(("dp", "ctx"), None),
        P(("dp", "ctx"), None),
        P("dp"),
    )
    out_specs = (
        P(("dp", "ctx"), None),
        P(("dp", "ctx"), None),
        P(("dp", "ctx"), None),
        P(("dp", "ctx"), None),
    )
    return jax.shard_map(choose, mesh=mesh, in_specs=in_specs, out_specs=out_specs, check_vma=False)
```

```python
import functools
import math

import jax
import jax.numpy as jnp
from jax import lax
from jax.experimental import pallas as pl
from jax.experimental.pallas import tpu as pltpu
from jax.sharding import PartitionSpec as P

HQ = 16
HK = 4
DH = 128
BLOCK = 64
CAP = 32


highest = lax.Precision.HIGHEST


def with_halo(array, sides, width):
    for axis, dim in sides:
        size, length = (lax.axis_size(axis), array.shape[dim])
        up = [(i, (i + 1) % size) for i in range(size - 1)]
        down = [(j, i) for i, j in up]
        last = lax.slice_in_dim(array, length - width, length, axis=dim)
        first = lax.slice_in_dim(array, 0, width, axis=dim)
        before = lax.ppermute(last, axis, up)
        after = lax.ppermute(first, axis, down)
        array = jnp.concatenate([before, array, after], axis=dim)
    return array


def combined_all(part, axis, combine):
    gathered = jax.tree.map(lambda a: lax.all_gather(a, axis), part)

    def take(source):
        return jax.tree.map(lambda a: lax.dynamic_index_in_dim(a, source, 0, False), gathered)

    return lax.fori_loop(
        1, lax.axis_size(axis), lambda source, state: combine(state, take(source)), take(0)
    )


def window_group(pieces, glob_keys, glob_values, score_scale):
    query_block, grad_block, key_window, value_window, key_usable, query_live = pieces
    near = (
        jnp.einsum("bqard,bkad->barqk", query_block, key_window, preferred_element_type=jnp.float32)
        * score_scale
    )
    far = (
        jnp.einsum("bqard,gad->barqg", query_block, glob_keys, preferred_element_type=jnp.float32)
        * score_scale
    )
    near = jnp.where(key_usable[:, None, None, None, :], near, -jnp.inf)
    row_top = jnp.maximum(jnp.max(near, axis=-1), jnp.max(far, axis=-1))
    near_weight = jnp.exp(near - row_top[..., None])
    far_weight = jnp.exp(far - row_top[..., None])
    total = jnp.sum(near_weight, axis=-1) + jnp.sum(far_weight, axis=-1)
    mixed = jnp.einsum(
        "barqk,bkad->bqard",
        near_weight.astype(jnp.bfloat16),
        value_window,
        preferred_element_type=jnp.float32,
    )
    mixed = mixed + jnp.einsum(
        "barqg,gad->bqard",
        far_weight.astype(jnp.bfloat16),
        glob_values,
        preferred_element_type=jnp.float32,
    )
    attended = mixed / jnp.transpose(total, (0, 3, 1, 2))[..., None]
    delta = jnp.transpose(jnp.sum(grad_block * attended, axis=-1), (0, 2, 3, 1))
    live = query_live[:, None, None, :, None]
    near_prob = near_weight / total[..., None]
    far_prob = far_weight / total[..., None]
    near_dprob = jnp.einsum(
        "bqard,bkad->barqk", grad_block, value_window, preferred_element_type=jnp.float32
    )
    far_dprob = jnp.einsum(
        "bqard,gad->barqg", grad_block, glob_values, preferred_element_type=jnp.float32
    )
    near_dscore = (near_prob * (near_dprob - delta[..., None]) * live).astype(jnp.bfloat16)
    far_dscore = (far_prob * (far_dprob - delta[..., None]) * live).astype(jnp.bfloat16)
    near_round = (near_prob * live).astype(jnp.bfloat16)
    far_round = (far_prob * live).astype(jnp.bfloat16)
    grad_query = jnp.einsum(
        "barqk,bkad->bqard", near_dscore, key_window, preferred_element_type=jnp.float32
    )
    grad_query = score_scale * (
        grad_query
        + jnp.einsum("barqg,gad->bqard", far_dscore, glob_keys, preferred_element_type=jnp.float32)
    )
    grad_key_win = score_scale * jnp.einsum(
        "barqk,bqard->bkad", near_dscore, query_block, preferred_element_type=jnp.float32
    )
    grad_value_win = jnp.einsum(
        "barqk,bqard->bkad", near_round, grad_block, preferred_element_type=jnp.float32
    )
    grad_key_glob = score_scale * jnp.einsum(
        "barqg,bqard->gad", far_dscore, query_block, preferred_element_type=jnp.float32
    )
    grad_value_glob = jnp.einsum(
        "barqg,bqard->gad", far_round, grad_block, preferred_element_type=jnp.float32
    )
    return (attended, grad_query, grad_key_win, grad_value_win, grad_key_glob, grad_value_glob)


def combine_softmax(left_part, right_part):
    left_top, left_total, left_summed = left_part
    right_top, right_total, right_summed = right_part
    joint_top = jnp.maximum(left_top, right_top)
    left_factor = jnp.exp(left_top - joint_top)
    right_factor = jnp.exp(right_top - joint_top)
    return (
        joint_top,
        left_total * left_factor + right_total * right_factor,
        left_summed * left_factor[..., None] + right_summed * right_factor[..., None],
    )


def local(queries, keys, values, grad_out, positions):
    tok_rows = queries.shape[0]
    query_width = queries.shape[1]
    key_width = keys.shape[1]
    q_per_kv = HQ // HK
    ctx_count = lax.axis_size("ctx")
    seq_total = tok_rows * ctx_count
    first_row = lax.axis_index("ctx") * tok_rows
    score_scale = 1.0 / math.sqrt(DH)
    glob_count = positions.shape[0]
    local_row = positions - first_row
    is_mine = (local_row >= 0) & (local_row < tok_rows)
    safe_row = jnp.clip(local_row, 0, tok_rows - 1)
    before = jnp.sum((positions < first_row).astype(jnp.int32))
    held_count = jnp.sum(is_mine.astype(jnp.int32))
    slot_index = jnp.arange(CAP)
    slot_ok = slot_index < held_count
    slot_row = jnp.clip(
        positions[jnp.clip(before + slot_index, 0, glob_count - 1)] - first_row, 0, tok_rows - 1
    )
    owner_index = positions // tok_rows
    owner_start = jnp.sum((owner_index[None, :] < owner_index[:, None]).astype(jnp.int32), axis=1)
    slot_of = owner_index * CAP + jnp.arange(glob_count) - owner_start
    packed = jnp.concatenate(
        [queries[slot_row], keys[slot_row], values[slot_row], grad_out[slot_row]], axis=1
    )
    packed = jnp.where(slot_ok[:, None], packed, jnp.zeros_like(packed))
    everyone = lax.all_gather(packed, "ctx", axis=0, tiled=True)
    compact = everyone[slot_of]
    glob_query = compact[:, :query_width].reshape(glob_count, HK, q_per_kv, DH)
    glob_keys = compact[:, query_width : query_width + key_width].reshape(glob_count, HK, DH)
    glob_values = compact[:, query_width + key_width : query_width + 2 * key_width].reshape(
        glob_count, HK, DH
    )
    glob_grad = compact[:, query_width + 2 * key_width :].reshape(glob_count, HK, q_per_kv, DH)
    paired = jnp.concatenate([keys, values], axis=1)
    extended = with_halo(paired, (("ctx", 0),), BLOCK)
    blocks = tok_rows // BLOCK
    ext_blocks = extended.reshape(blocks + 2, BLOCK, 2 * key_width)
    window = jnp.concatenate([ext_blocks[:-2], ext_blocks[1:-1], ext_blocks[2:]], axis=1)
    key_window = window[:, :, :key_width].reshape(blocks, 3 * BLOCK, HK, DH)
    value_window = window[:, :, key_width:].reshape(blocks, 3 * BLOCK, HK, DH)
    ext_position = first_row - BLOCK + jnp.arange(tok_rows + 2 * BLOCK)
    ext_global = jnp.any(ext_position[:, None] == positions[None, :], axis=1)
    ext_usable = (
        (ext_position >= 0) & (ext_position < seq_total) & jnp.logical_not(ext_global)
    ).reshape(blocks + 2, BLOCK)
    key_usable = jnp.concatenate([ext_usable[:-2], ext_usable[1:-1], ext_usable[2:]], axis=1)
    query_live = (
        jnp.logical_not(ext_global[BLOCK : BLOCK + tok_rows])
        .astype(jnp.float32)
        .reshape(blocks, BLOCK)
    )
    per_step = min(8, blocks)
    step_count = blocks // per_step

    def regroup(source):
        return source.reshape((step_count, per_step) + source.shape[1:])

    stacked = (
        regroup(queries.reshape(blocks, BLOCK, HK, q_per_kv, DH)),
        regroup(grad_out.reshape(blocks, BLOCK, HK, q_per_kv, DH)),
        regroup(key_window),
        regroup(value_window),
        regroup(key_usable),
        regroup(query_live),
    )
    results = lax.map(
        lambda pieces: window_group(pieces, glob_keys, glob_values, score_scale), stacked
    )
    attended_loc = results[0].reshape(tok_rows, query_width)
    grad_query_loc = results[1].reshape(tok_rows, query_width)
    window_grads = jnp.concatenate(
        [
            results[2].reshape(blocks, 3, BLOCK, key_width),
            results[3].reshape(blocks, 3, BLOCK, key_width),
        ],
        axis=3,
    )
    glob_key_grad = jnp.sum(results[4], axis=0).reshape(glob_count, key_width)
    glob_value_grad = jnp.sum(results[5], axis=0).reshape(glob_count, key_width)
    key_here = keys.reshape(tok_rows, HK, DH)
    value_here = values.reshape(tok_rows, HK, DH)
    glob_score = (
        jnp.einsum("gard,uad->argu", glob_query, key_here, preferred_element_type=jnp.float32)
        * score_scale
    )
    top_here = jnp.max(glob_score, axis=-1)
    weight_here = jnp.exp(glob_score - top_here[..., None])
    total_here = jnp.sum(weight_here, axis=-1)
    summed_here = jnp.einsum(
        "argu,uad->argd", weight_here, value_here.astype(jnp.float32), precision=highest
    )
    glob_top, glob_total, glob_summed = combined_all(
        (top_here, total_here, summed_here), "ctx", combine_softmax
    )
    glob_attended = glob_summed / glob_total[..., None]
    glob_delta = jnp.sum(
        jnp.transpose(glob_grad, (1, 2, 0, 3)).astype(jnp.float32) * glob_attended, axis=-1
    )
    glob_prob = jnp.exp(glob_score - glob_top[..., None]) / glob_total[..., None]
    glob_dprob = jnp.einsum(
        "gard,uad->argu", glob_grad, value_here, preferred_element_type=jnp.float32
    )
    glob_dscore = (glob_prob * (glob_dprob - glob_delta[..., None])).astype(jnp.bfloat16)
    glob_round = glob_prob.astype(jnp.bfloat16)
    glob_query_grad = score_scale * jnp.einsum(
        "argu,uad->gard", glob_dscore, key_here, preferred_element_type=jnp.float32
    )
    key_grad_here = score_scale * jnp.einsum(
        "argu,gard->uad", glob_dscore, glob_query, preferred_element_type=jnp.float32
    )
    value_grad_here = jnp.einsum(
        "argu,gard->uad", glob_round, glob_grad, preferred_element_type=jnp.float32
    )
    empty_block = jnp.zeros((1, BLOCK, 2 * key_width), jnp.float32)
    spread = jnp.concatenate([window_grads[:, 0], empty_block, empty_block], axis=0)
    spread = spread + jnp.concatenate([empty_block, window_grads[:, 1], empty_block], axis=0)
    spread = spread + jnp.concatenate([empty_block, empty_block, window_grads[:, 2]], axis=0)
    rims = jnp.concatenate([spread[0], spread[-1]], axis=0)
    arrived = with_halo(rims, (("ctx", 0),), BLOCK)
    pair_grad = spread[1:-1].reshape(tok_rows, 2 * key_width)
    pair_grad = pair_grad.at[:BLOCK].add(arrived[:BLOCK])
    pair_grad = pair_grad.at[tok_rows - BLOCK :].add(arrived[3 * BLOCK :])
    pair_grad = pair_grad + jnp.concatenate(
        [key_grad_here.reshape(tok_rows, key_width), value_grad_here.reshape(tok_rows, key_width)],
        axis=1,
    )
    glob_grads = jnp.concatenate(
        [glob_query_grad.reshape(glob_count, query_width), glob_key_grad, glob_value_grad], axis=1
    )
    laid = (
        jnp.zeros((ctx_count * CAP, glob_grads.shape[1]), jnp.float32).at[slot_of].set(glob_grads)
    )
    returned = lax.psum_scatter(laid, "ctx", scatter_dimension=0, tiled=True)
    target = jnp.where(slot_ok, slot_row, tok_rows)
    grad_query_all = grad_query_loc.at[target].add(returned[:, :query_width], mode="drop")
    pair_grad = pair_grad.at[target].add(returned[:, query_width:], mode="drop")
    glob_rows_out = jnp.transpose(glob_attended, (2, 0, 1, 3)).reshape(glob_count, query_width)
    attended_all = attended_loc.at[jnp.where(is_mine, safe_row, tok_rows)].set(
        glob_rows_out, mode="drop"
    )
    return (
        attended_all.astype(jnp.bfloat16),
        grad_query_all.astype(jnp.bfloat16),
        pair_grad[:, :key_width].astype(jnp.bfloat16),
        pair_grad[:, key_width:].astype(jnp.bfloat16),
    )


MESH = pl.DeviceIdType.MESH
ROWS = 4
REP = HQ // HK
TOK = 128
FAR = -1e30


def dense_kernel(
    pos_row, q_in, k_in, v_in, g_in,
    att_out, gq_out, gk_ref, gv_ref,
    q_ref, g_ref, att_ref, gq_ref,
    kbuf, vbuf, qt, gt, qs, gs, sbuf, dbuf, pbuf, wbuf, top8, total8, mixed8,
    acc, xsend, xrecv, csend, crecv, erecv,
    in_s, out_s, ax_s, ax_r, au_s, au_r, ad_s, ad_r, ek_s, ek_r, rx_s, rx_r, rc_s, rc_r, ex_s, ex_r,
):
    c = lax.axis_index("ctx")
    z, x = c // 2, c % 2
    partner = c + 1 - 2 * x
    scale = 1.0 / math.sqrt(DH)
    own = (k_in, v_in)
    bufs = (kbuf, vbuf)
    wide = REP * TOK

    def rows(block):
        return pl.ds(pl.multiple_of(block * TOK, TOK), TOK)

    def head(j):
        return pl.ds(pl.multiple_of(j * DH, DH), DH)

    loads = [
        pltpu.make_async_copy(source, target, in_s.at[i])
        for i, (source, target) in enumerate(
            ((k_in, kbuf.at[rows(c)]), (v_in, vbuf.at[rows(c)]), (q_in, q_ref), (g_in, g_ref))
        )
    ]
    for load in loads:
        load.start()

    barrier = pltpu.get_barrier_semaphore()
    pl.semaphore_signal(barrier, inc=1, device_id={"ctx": partner}, device_id_type=MESH)

    @pl.when(z > 0)
    def _():
        pl.semaphore_signal(barrier, inc=1, device_id={"ctx": c - 2}, device_id_type=MESH)

    @pl.when(z < ROWS - 1)
    def _():
        pl.semaphore_signal(barrier, inc=1, device_id={"ctx": c + 2}, device_id_type=MESH)

    pl.semaphore_wait(
        barrier, 1 + (z > 0).astype(jnp.int32) + (z < ROWS - 1).astype(jnp.int32)
    )

    def remote(source, target, send, recv, device):
        return pltpu.make_async_remote_copy(
            src_ref=source, dst_ref=target, send_sem=send, recv_sem=recv,
            device_id={"ctx": device}, device_id_type=MESH,
        )

    def along(h, k, up, source=None):
        block = c - 2 * (k - 1) if up else c + 2 * (k - 1)
        here = bufs[h].at[rows(block)]
        send, recv = (au_s, au_r) if up else (ad_s, ad_r)
        return remote(
            here if source is None else source, here,
            send.at[h, k - 1], recv.at[h, k - 1], c + 2 if up else c - 2,
        )

    def along_in(h, k, up):
        block = c - 2 * k if up else c + 2 * k
        here = bufs[h].at[rows(block)]
        send, recv = (au_s, au_r) if up else (ad_s, ad_r)
        return remote(here, here, send.at[h, k - 1], recv.at[h, k - 1], partner)

    def across(h, zz, source=None):
        here = bufs[h].at[rows(2 * zz + x)]
        return remote(
            here if source is None else source, here, ax_s.at[h, zz], ax_r.at[h, zz], partner
        )

    def across_in(h, zz):
        here = bufs[h].at[rows(2 * zz + 1 - x)]
        return remote(here, here, ax_s.at[h, zz], ax_r.at[h, zz], partner)

    for h in (0, 1):
        across(h, z, own[h]).start()

        @pl.when(z < ROWS - 1)
        def _():
            along(h, 1, True, own[h]).start()

        @pl.when(z > 0)
        def _():
            along(h, 1, False, own[h]).start()

    def beside(up):
        here = kbuf.at[rows(2 * z + 1 - x)]
        i = 0 if up else 1
        return remote(here, here, ek_s.at[i], ek_r.at[i], c + 2 if up else c - 2)

    def beside_in(up):
        here = kbuf.at[rows(2 * (z - 1 if up else z + 1) + 1 - x)]
        i = 0 if up else 1
        return remote(here, here, ek_s.at[i], ek_r.at[i], partner)

    for load in loads:
        load.wait()

    def stack(j, carry):
        for r in range(REP):
            cols = pl.ds(pl.multiple_of((j * REP + r) * DH, DH), DH)
            part = q_ref[:, cols]
            qs[j, r * TOK : (r + 1) * TOK, :] = part
            qt[j, :, r * TOK : (r + 1) * TOK] = part.astype(jnp.float32).T.astype(jnp.bfloat16)
            part = g_ref[:, cols]
            gs[j, r * TOK : (r + 1) * TOK, :] = part
            gt[j, :, r * TOK : (r + 1) * TOK] = part.astype(jnp.float32).T.astype(jnp.bfloat16)
        return carry

    lax.fori_loop(0, HK, stack, 0)
    top8[...] = jnp.full(top8.shape, FAR, jnp.float32)
    total8[...] = jnp.zeros(total8.shape, jnp.float32)
    mixed8[...] = jnp.zeros(mixed8.shape, jnp.float32)

    glob_count = pos_row.shape[1]

    def is_glob(block):
        token = block * TOK + lax.broadcasted_iota(jnp.int32, (TOK, glob_count), 0)
        return jnp.max(jnp.where(pos_row[...] == token, 1.0, 0.0), axis=1, keepdims=True)

    row_glob = jnp.broadcast_to(is_glob(c), (TOK, TOK)).T

    def block_bias(block):
        col_glob = is_glob(block)
        u_block = block * (TOK // BLOCK) + lax.broadcasted_iota(jnp.int32, (TOK, TOK), 0) // BLOCK
        t_block = c * (TOK // BLOCK) + lax.broadcasted_iota(jnp.int32, (TOK, TOK), 1) // BLOCK
        near = jnp.where(jnp.abs(u_block - t_block) <= 1, 1.0, 0.0)
        allowed = jnp.maximum(jnp.maximum(near, row_glob), col_glob)
        bias = jnp.where(allowed > 0.5, 0.0, FAR)
        return jnp.concatenate([bias] * REP, axis=1)

    def scores(block):
        bias = block_bias(block)
        at = rows(block)

        for j in range(HK):
            cols = slice(j * DH, (j + 1) * DH)
            s = jnp.dot(kbuf[at, cols], qt[j], preferred_element_type=jnp.float32)
            s = s * scale + bias
            sbuf[j, at, :] = s
            d = jnp.dot(vbuf[at, cols], gt[j], preferred_element_type=jnp.float32)
            dbuf[j, at, :] = d
            s = s.reshape(TOK // 8, 8, wide)
            old = top8[j]
            new = jnp.maximum(old, jnp.max(s, axis=0))
            factor = jnp.exp(old - new)
            e = jnp.exp(s - new[None])
            top8[j] = new
            total8[j] = total8[j] * factor + jnp.sum(e, axis=0)
            e = e * d.reshape(TOK // 8, 8, wide)
            mixed8[j] = mixed8[j] * factor + jnp.sum(e, axis=0)

    scores(c)
    across_in(0, z).wait_recv()

    @pl.when(z < ROWS - 1)
    def _():
        beside(True).start()

    @pl.when(z > 0)
    def _():
        beside(False).start()

    def gather_step(k, carry):
        @pl.when(z - k >= 0)
        def _():
            for h in (0, 1):
                along_in(h, k, True).wait_recv()

                @pl.when(z < ROWS - 1)
                def _():
                    along(h, k + 1, True).start()

                if h == 0:

                    @pl.when(k > 1)
                    def _():
                        across(0, z - k).start()

                else:
                    across(1, z - k).start()

        @pl.when(z + k < ROWS)
        def _():
            for h in (0, 1):
                along_in(h, k, False).wait_recv()

                @pl.when(z > 0)
                def _():
                    along(h, k + 1, False).start()

                if h == 0:

                    @pl.when(k > 1)
                    def _():
                        across(0, z + k).start()

                else:
                    across(1, z + k).start()

        @pl.when(z - k >= 0)
        def _():
            scores(c - 2 * k)

        @pl.when(z + k < ROWS)
        def _():
            scores(c + 2 * k)

        @pl.when(z - (k - 1) >= 0)
        def _():
            @pl.when(k == 2)
            def _():
                beside_in(True).wait_recv()

            @pl.when(k > 2)
            def _():
                across_in(0, z - (k - 1)).wait_recv()

            across_in(1, z - (k - 1)).wait_recv()
            scores(2 * (z - (k - 1)) + 1 - x)

        @pl.when((z + (k - 1) < ROWS) & (k > 1))
        def _():
            @pl.when(k == 2)
            def _():
                beside_in(False).wait_recv()

            @pl.when(k > 2)
            def _():
                across_in(0, z + (k - 1)).wait_recv()

            across_in(1, z + (k - 1)).wait_recv()
            scores(2 * (z + (k - 1)) + 1 - x)

        return carry

    lax.fori_loop(1, ROWS + 1, gather_step, 0)

    for j in range(HK):
        top = jnp.max(top8[j], axis=0, keepdims=True)
        factor = jnp.exp(top8[j] - top)
        reciprocal = 1.0 / jnp.sum(total8[j] * factor, axis=0, keepdims=True)
        delta = jnp.sum(mixed8[j] * factor, axis=0, keepdims=True) * reciprocal
        top8[j] = jnp.broadcast_to(top, (8, wide))
        total8[j] = jnp.broadcast_to(reciprocal, (8, wide))
        mixed8[j] = jnp.broadcast_to(delta, (8, wide))

    def terms(block, out):
        at = rows(block)

        for j in range(HK):
            cols = slice(j * DH, (j + 1) * DH)
            p = jnp.exp(sbuf[j, at, :] - top8[j, 0:1, :]) * total8[j, 0:1, :]
            w = (p * (dbuf[j, at, :] - mixed8[j, 0:1, :])).astype(jnp.bfloat16)
            p = p.astype(jnp.bfloat16)
            pbuf[j, at, :] = p
            wbuf[j, at, :] = w
            dk = jnp.dot(w, qs[j], preferred_element_type=jnp.float32) * scale
            dv = jnp.dot(p, gs[j], preferred_element_type=jnp.float32)
            out[0, :, cols] = dk.astype(out.dtype)
            out[1, :, cols] = dv.astype(out.dtype)

    def pick(a, b, d, e):
        return jnp.where(z == 0, a, jnp.where(z == 1, b, jnp.where(z == 2, d, e)))

    order = (pick(3, 3, 0, 0), pick(2, 0, 3, 1), pick(1, 2, 1, 2), z)

    def cross(h, o):
        return remote(
            xsend.at[o, h], xrecv.at[o, h], rx_s.at[h, o], rx_r.at[h, o], partner
        )

    near = (None, (z == 1) | (z == 2), None, None)

    def extra(o):
        down = order[o] < z
        i = jnp.where(down, 1, 0)
        return remote(
            xsend.at[o, 0], erecv.at[i], ex_s.at[i], ex_r.at[i], jnp.where(down, c - 2, c + 2)
        )

    def extra_in(i):
        return remote(erecv.at[i], erecv.at[i], ex_s.at[i], ex_r.at[i], partner)

    def phase(o):
        terms(2 * order[o] + 1 - x, xsend.at[o])
        if o == 2:
            extra(2).start()
        elif o == 1:

            @pl.when(near[1])
            def _():
                extra(1).start()

            @pl.when(jnp.logical_not(near[1]))
            def _():
                cross(0, 1).start()

        elif o == 3:

            @pl.when(z > 0)
            def _():
                extra_in(0).wait_recv()
                both = xsend[3, 0].astype(jnp.float32) + erecv[0].astype(jnp.float32)
                xsend[3, 0] = both.astype(jnp.bfloat16)

            @pl.when(z < ROWS - 1)
            def _():
                extra_in(1).wait_recv()
                both = xsend[3, 0].astype(jnp.float32) + erecv[1].astype(jnp.float32)
                xsend[3, 0] = both.astype(jnp.bfloat16)

            cross(0, 3).start()
        else:
            cross(0, 0).start()
        cross(1, o).start()
        terms(2 * order[o] + x, acc.at[o])

    def chain(h, o):
        down = order[o] < z
        to = jnp.where(down, z - 1, z + 1)
        slot = jnp.where((to == order[o]) & jnp.logical_not(down), ROWS, order[o])
        return remote(
            csend.at[o, h], crecv.at[slot, h], rc_s.at[h, o], rc_r.at[h, slot], 2 * to + x
        )

    def chain_in(h, slot):
        return remote(crecv.at[slot, h], crecv.at[slot, h], rc_s.at[h, 0], rc_r.at[h, slot], partner)

    def pass_on(o, h):
        down = order[o] < z
        fed = (down & (z < ROWS - 1)) | (jnp.logical_not(down) & (z > 0))

        def add_crossed():
            cross(h, o).wait_recv()
            acc[o, h] = acc[o, h] + xrecv[o, h].astype(jnp.float32)

        if h == 1 or o == 0:
            add_crossed()
        elif o == 1:
            pl.when(jnp.logical_not(near[1]))(add_crossed)

        @pl.when(fed)
        def _():
            chain_in(h, order[o]).wait_recv()
            acc[o, h] = acc[o, h] + crecv[order[o], h].astype(jnp.float32)

        csend[o, h] = acc[o, h].astype(jnp.bfloat16)
        chain(h, o).start()

    edge = (z == 0) | (z == ROWS - 1)
    phase(0)
    phase(1)
    pass_on(0, 0)
    phase(2)

    @pl.when(edge)
    def _():
        pass_on(2, 0)

    pass_on(0, 1)
    phase(3)

    def outputs(j, carry):
        across_rows = (((0,), (0,)), ((), ()))
        mixed = lax.dot_general(
            vbuf[:, head(j)], pbuf[j], across_rows, preferred_element_type=jnp.float32
        )
        grad = scale * lax.dot_general(
            kbuf[:, head(j)], wbuf[j], across_rows, preferred_element_type=jnp.float32
        )
        for r in range(REP):
            cols = pl.ds(pl.multiple_of((j * REP + r) * DH, DH), DH)
            att_ref[:, cols] = mixed[:, r * TOK : (r + 1) * TOK].T.astype(jnp.bfloat16)
            gq_ref[:, cols] = grad[:, r * TOK : (r + 1) * TOK].T.astype(jnp.bfloat16)
        return carry

    lax.fori_loop(0, HK // 2, outputs, 0)
    pass_on(1, 0)
    lax.fori_loop(HK // 2, HK, outputs, 0)
    stores = [
        pltpu.make_async_copy(att_ref, att_out, out_s.at[0]),
        pltpu.make_async_copy(gq_ref, gq_out, out_s.at[1]),
    ]
    for store in stores:
        store.start()
    pass_on(1, 1)

    @pl.when(jnp.logical_not(edge))
    def _():
        pass_on(2, 0)

    pass_on(2, 1)
    last = ROWS - 1
    for h, out in ((0, gk_ref), (1, gv_ref)):
        cross(h, last).wait_recv()
        acc[last, h] = acc[last, h] + xrecv[last, h].astype(jnp.float32)

        @pl.when(z < ROWS - 1)
        def _():
            chain_in(h, z).wait_recv()
            acc[last, h] = acc[last, h] + crecv[z, h].astype(jnp.float32)

        @pl.when(z > 0)
        def _():
            chain_in(h, ROWS).wait_recv()
            acc[last, h] = acc[last, h] + crecv[ROWS, h].astype(jnp.float32)

        out[...] = acc[last, h].astype(jnp.bfloat16)

    for store in stores:
        store.wait()
    across(0, z).wait_send()
    for h in (0, 1):
        cross(h, 0).wait_send()
        cross(h, 3).wait_send()
    cross(1, 1).wait_send()
    cross(1, 2).wait_send()
    extra(2).wait_send()

    @pl.when(near[1])
    def _():
        extra(1).wait_send()

    @pl.when(jnp.logical_not(near[1]))
    def _():
        cross(0, 1).wait_send()

    @pl.when(z < ROWS - 1)
    def _():
        beside(True).wait_send()

    @pl.when(z > 0)
    def _():
        beside(False).wait_send()

    for zz in range(ROWS):
        across(1, zz).wait_send()

        @pl.when(jnp.abs(z - zz) > 1)
        def _():
            across(0, zz).wait_send()

    for h in (0, 1):
        for o in range(ROWS - 1):
            chain(h, o).wait_send()
        for k in range(1, ROWS):

            @pl.when((z - (k - 1) >= 0) & (z < ROWS - 1))
            def _():
                along(h, k, True).wait_send()

            @pl.when((z + (k - 1) < ROWS) & (z > 0))
            def _():
                along(h, k, False).wait_send()


def copy_kernel(*refs):
    sems = refs[-1]
    count = len(refs) // 2
    copies = [
        pltpu.make_async_copy(refs[i], refs[count + i], sems.at[i]) for i in range(count)
    ]
    for copy in copies:
        copy.start()
    for copy in copies:
        copy.wait()


def dense(queries, keys, values, grad_out, positions):
    tokens = TOK * 2 * ROWS
    key_width = HK * DH
    wide = REP * TOK
    bf16, f32 = jnp.bfloat16, jnp.float32
    vmem = pl.BlockSpec(memory_space=pltpu.VMEM)
    dma = pltpu.SemaphoreType.DMA
    anywhere = pl.BlockSpec(memory_space=pl.ANY)
    shapes = [
        jax.ShapeDtypeStruct((TOK, HQ * DH), bf16),
        jax.ShapeDtypeStruct((TOK, HQ * DH), bf16),
        jax.ShapeDtypeStruct((TOK, key_width), bf16),
        jax.ShapeDtypeStruct((TOK, key_width), bf16),
    ]
    results = pl.pallas_call(
        dense_kernel,
        out_shape=shapes,
        in_specs=[vmem] + [anywhere] * 4,
        out_specs=[anywhere] * 2 + [vmem] * 2,
        scratch_shapes=[
            pltpu.VMEM((TOK, HQ * DH), bf16),
            pltpu.VMEM((TOK, HQ * DH), bf16),
            pltpu.VMEM((TOK, HQ * DH), bf16),
            pltpu.VMEM((TOK, HQ * DH), bf16),
            pltpu.VMEM((tokens, key_width), bf16),
            pltpu.VMEM((tokens, key_width), bf16),
            pltpu.VMEM((HK, DH, wide), bf16),
            pltpu.VMEM((HK, DH, wide), bf16),
            pltpu.VMEM((HK, wide, DH), bf16),
            pltpu.VMEM((HK, wide, DH), bf16),
            pltpu.VMEM((HK, tokens, wide), f32),
            pltpu.VMEM((HK, tokens, wide), f32),
            pltpu.VMEM((HK, tokens, wide), bf16),
            pltpu.VMEM((HK, tokens, wide), bf16),
            pltpu.VMEM((HK, 8, wide), f32),
            pltpu.VMEM((HK, 8, wide), f32),
            pltpu.VMEM((HK, 8, wide), f32),
            pltpu.VMEM((ROWS, 2, TOK, key_width), f32),
            pltpu.VMEM((ROWS, 2, TOK, key_width), bf16),
            pltpu.VMEM((ROWS, 2, TOK, key_width), bf16),
            pltpu.VMEM((ROWS - 1, 2, TOK, key_width), bf16),
            pltpu.VMEM((ROWS + 1, 2, TOK, key_width), bf16),
            pltpu.VMEM((2, TOK, key_width), bf16),
            dma((4,)),
            dma((2,)),
            dma((2, ROWS)),
            dma((2, ROWS)),
            dma((2, ROWS - 1)),
            dma((2, ROWS - 1)),
            dma((2, ROWS - 1)),
            dma((2, ROWS - 1)),
            dma((2,)),
            dma((2,)),
            dma((2, ROWS)),
            dma((2, ROWS)),
            dma((2, ROWS - 1)),
            dma((2, ROWS + 1)),
            dma((2,)),
            dma((2,)),
        ],
        compiler_params=pltpu.CompilerParams(
            collective_id=0, has_side_effects=True, vmem_limit_bytes=56 * 1024 * 1024
        ),
    )(positions.reshape(1, -1), queries, keys, values, grad_out)
    return pl.pallas_call(
        copy_kernel,
        out_shape=shapes,
        in_specs=[anywhere] * 4,
        out_specs=[anywhere] * 4,
        scratch_shapes=[dma((4,))],
    )(*results)


def choose(queries, keys, values, grad_out, positions):
    if lax.axis_size("ctx") == 2 * ROWS and queries.shape[0] == TOK:
        return tuple(dense(queries, keys, values, grad_out, positions))
    return local(queries, keys, values, grad_out, positions)


def solution(mesh):
    in_specs = (
        P(("dp", "ctx"), None),
        P(("dp", "ctx"), None),
        P(("dp", "ctx"), None),
        P(("dp", "ctx"), None),
        P("dp"),
    )
    out_specs = (
        P(("dp", "ctx"), None),
        P(("dp", "ctx"), None),
        P(("dp", "ctx"), None),
        P(("dp", "ctx"), None),
    )
    return jax.shard_map(choose, mesh=mesh, in_specs=in_specs, out_specs=out_specs, check_vma=False)
```

```python
import functools
import math

import jax
import jax.numpy as jnp
from jax import lax
from jax.experimental import pallas as pl
from jax.experimental.pallas import tpu as pltpu
from jax.sharding import PartitionSpec as P

HQ = 16
HK = 4
DH = 128
BLOCK = 64
CAP = 32


highest = lax.Precision.HIGHEST


def with_halo(array, sides, width):
    for axis, dim in sides:
        size, length = (lax.axis_size(axis), array.shape[dim])
        up = [(i, (i + 1) % size) for i in range(size - 1)]
        down = [(j, i) for i, j in up]
        last = lax.slice_in_dim(array, length - width, length, axis=dim)
        first = lax.slice_in_dim(array, 0, width, axis=dim)
        before = lax.ppermute(last, axis, up)
        after = lax.ppermute(first, axis, down)
        array = jnp.concatenate([before, array, after], axis=dim)
    return array


def combined_all(part, axis, combine):
    gathered = jax.tree.map(lambda a: lax.all_gather(a, axis), part)

    def take(source):
        return jax.tree.map(lambda a: lax.dynamic_index_in_dim(a, source, 0, False), gathered)

    return lax.fori_loop(
        1, lax.axis_size(axis), lambda source, state: combine(state, take(source)), take(0)
    )


def window_group(pieces, glob_keys, glob_values, score_scale):
    query_block, grad_block, key_window, value_window, key_usable, query_live = pieces
    near = (
        jnp.einsum("bqard,bkad->barqk", query_block, key_window, preferred_element_type=jnp.float32)
        * score_scale
    )
    far = (
        jnp.einsum("bqard,gad->barqg", query_block, glob_keys, preferred_element_type=jnp.float32)
        * score_scale
    )
    near = jnp.where(key_usable[:, None, None, None, :], near, -jnp.inf)
    row_top = jnp.maximum(jnp.max(near, axis=-1), jnp.max(far, axis=-1))
    near_weight = jnp.exp(near - row_top[..., None])
    far_weight = jnp.exp(far - row_top[..., None])
    total = jnp.sum(near_weight, axis=-1) + jnp.sum(far_weight, axis=-1)
    mixed = jnp.einsum(
        "barqk,bkad->bqard",
        near_weight.astype(jnp.bfloat16),
        value_window,
        preferred_element_type=jnp.float32,
    )
    mixed = mixed + jnp.einsum(
        "barqg,gad->bqard",
        far_weight.astype(jnp.bfloat16),
        glob_values,
        preferred_element_type=jnp.float32,
    )
    attended = mixed / jnp.transpose(total, (0, 3, 1, 2))[..., None]
    delta = jnp.transpose(jnp.sum(grad_block * attended, axis=-1), (0, 2, 3, 1))
    live = query_live[:, None, None, :, None]
    near_prob = near_weight / total[..., None]
    far_prob = far_weight / total[..., None]
    near_dprob = jnp.einsum(
        "bqard,bkad->barqk", grad_block, value_window, preferred_element_type=jnp.float32
    )
    far_dprob = jnp.einsum(
        "bqard,gad->barqg", grad_block, glob_values, preferred_element_type=jnp.float32
    )
    near_dscore = (near_prob * (near_dprob - delta[..., None]) * live).astype(jnp.bfloat16)
    far_dscore = (far_prob * (far_dprob - delta[..., None]) * live).astype(jnp.bfloat16)
    near_round = (near_prob * live).astype(jnp.bfloat16)
    far_round = (far_prob * live).astype(jnp.bfloat16)
    grad_query = jnp.einsum(
        "barqk,bkad->bqard", near_dscore, key_window, preferred_element_type=jnp.float32
    )
    grad_query = score_scale * (
        grad_query
        + jnp.einsum("barqg,gad->bqard", far_dscore, glob_keys, preferred_element_type=jnp.float32)
    )
    grad_key_win = score_scale * jnp.einsum(
        "barqk,bqard->bkad", near_dscore, query_block, preferred_element_type=jnp.float32
    )
    grad_value_win = jnp.einsum(
        "barqk,bqard->bkad", near_round, grad_block, preferred_element_type=jnp.float32
    )
    grad_key_glob = score_scale * jnp.einsum(
        "barqg,bqard->gad", far_dscore, query_block, preferred_element_type=jnp.float32
    )
    grad_value_glob = jnp.einsum(
        "barqg,bqard->gad", far_round, grad_block, preferred_element_type=jnp.float32
    )
    return (attended, grad_query, grad_key_win, grad_value_win, grad_key_glob, grad_value_glob)


def combine_softmax(left_part, right_part):
    left_top, left_total, left_summed = left_part
    right_top, right_total, right_summed = right_part
    joint_top = jnp.maximum(left_top, right_top)
    left_factor = jnp.exp(left_top - joint_top)
    right_factor = jnp.exp(right_top - joint_top)
    return (
        joint_top,
        left_total * left_factor + right_total * right_factor,
        left_summed * left_factor[..., None] + right_summed * right_factor[..., None],
    )


def local(queries, keys, values, grad_out, positions):
    tok_rows = queries.shape[0]
    query_width = queries.shape[1]
    key_width = keys.shape[1]
    q_per_kv = HQ // HK
    ctx_count = lax.axis_size("ctx")
    seq_total = tok_rows * ctx_count
    first_row = lax.axis_index("ctx") * tok_rows
    score_scale = 1.0 / math.sqrt(DH)
    glob_count = positions.shape[0]
    local_row = positions - first_row
    is_mine = (local_row >= 0) & (local_row < tok_rows)
    safe_row = jnp.clip(local_row, 0, tok_rows - 1)
    before = jnp.sum((positions < first_row).astype(jnp.int32))
    held_count = jnp.sum(is_mine.astype(jnp.int32))
    slot_index = jnp.arange(CAP)
    slot_ok = slot_index < held_count
    slot_row = jnp.clip(
        positions[jnp.clip(before + slot_index, 0, glob_count - 1)] - first_row, 0, tok_rows - 1
    )
    owner_index = positions // tok_rows
    owner_start = jnp.sum((owner_index[None, :] < owner_index[:, None]).astype(jnp.int32), axis=1)
    slot_of = owner_index * CAP + jnp.arange(glob_count) - owner_start
    packed = jnp.concatenate(
        [queries[slot_row], keys[slot_row], values[slot_row], grad_out[slot_row]], axis=1
    )
    packed = jnp.where(slot_ok[:, None], packed, jnp.zeros_like(packed))
    everyone = lax.all_gather(packed, "ctx", axis=0, tiled=True)
    compact = everyone[slot_of]
    glob_query = compact[:, :query_width].reshape(glob_count, HK, q_per_kv, DH)
    glob_keys = compact[:, query_width : query_width + key_width].reshape(glob_count, HK, DH)
    glob_values = compact[:, query_width + key_width : query_width + 2 * key_width].reshape(
        glob_count, HK, DH
    )
    glob_grad = compact[:, query_width + 2 * key_width :].reshape(glob_count, HK, q_per_kv, DH)
    paired = jnp.concatenate([keys, values], axis=1)
    extended = with_halo(paired, (("ctx", 0),), BLOCK)
    blocks = tok_rows // BLOCK
    ext_blocks = extended.reshape(blocks + 2, BLOCK, 2 * key_width)
    window = jnp.concatenate([ext_blocks[:-2], ext_blocks[1:-1], ext_blocks[2:]], axis=1)
    key_window = window[:, :, :key_width].reshape(blocks, 3 * BLOCK, HK, DH)
    value_window = window[:, :, key_width:].reshape(blocks, 3 * BLOCK, HK, DH)
    ext_position = first_row - BLOCK + jnp.arange(tok_rows + 2 * BLOCK)
    ext_global = jnp.any(ext_position[:, None] == positions[None, :], axis=1)
    ext_usable = (
        (ext_position >= 0) & (ext_position < seq_total) & jnp.logical_not(ext_global)
    ).reshape(blocks + 2, BLOCK)
    key_usable = jnp.concatenate([ext_usable[:-2], ext_usable[1:-1], ext_usable[2:]], axis=1)
    query_live = (
        jnp.logical_not(ext_global[BLOCK : BLOCK + tok_rows])
        .astype(jnp.float32)
        .reshape(blocks, BLOCK)
    )
    per_step = min(8, blocks)
    step_count = blocks // per_step

    def regroup(source):
        return source.reshape((step_count, per_step) + source.shape[1:])

    stacked = (
        regroup(queries.reshape(blocks, BLOCK, HK, q_per_kv, DH)),
        regroup(grad_out.reshape(blocks, BLOCK, HK, q_per_kv, DH)),
        regroup(key_window),
        regroup(value_window),
        regroup(key_usable),
        regroup(query_live),
    )
    results = lax.map(
        lambda pieces: window_group(pieces, glob_keys, glob_values, score_scale), stacked
    )
    attended_loc = results[0].reshape(tok_rows, query_width)
    grad_query_loc = results[1].reshape(tok_rows, query_width)
    window_grads = jnp.concatenate(
        [
            results[2].reshape(blocks, 3, BLOCK, key_width),
            results[3].reshape(blocks, 3, BLOCK, key_width),
        ],
        axis=3,
    )
    glob_key_grad = jnp.sum(results[4], axis=0).reshape(glob_count, key_width)
    glob_value_grad = jnp.sum(results[5], axis=0).reshape(glob_count, key_width)
    key_here = keys.reshape(tok_rows, HK, DH)
    value_here = values.reshape(tok_rows, HK, DH)
    glob_score = (
        jnp.einsum("gard,uad->argu", glob_query, key_here, preferred_element_type=jnp.float32)
        * score_scale
    )
    top_here = jnp.max(glob_score, axis=-1)
    weight_here = jnp.exp(glob_score - top_here[..., None])
    total_here = jnp.sum(weight_here, axis=-1)
    summed_here = jnp.einsum(
        "argu,uad->argd", weight_here, value_here.astype(jnp.float32), precision=highest
    )
    glob_top, glob_total, glob_summed = combined_all(
        (top_here, total_here, summed_here), "ctx", combine_softmax
    )
    glob_attended = glob_summed / glob_total[..., None]
    glob_delta = jnp.sum(
        jnp.transpose(glob_grad, (1, 2, 0, 3)).astype(jnp.float32) * glob_attended, axis=-1
    )
    glob_prob = jnp.exp(glob_score - glob_top[..., None]) / glob_total[..., None]
    glob_dprob = jnp.einsum(
        "gard,uad->argu", glob_grad, value_here, preferred_element_type=jnp.float32
    )
    glob_dscore = (glob_prob * (glob_dprob - glob_delta[..., None])).astype(jnp.bfloat16)
    glob_round = glob_prob.astype(jnp.bfloat16)
    glob_query_grad = score_scale * jnp.einsum(
        "argu,uad->gard", glob_dscore, key_here, preferred_element_type=jnp.float32
    )
    key_grad_here = score_scale * jnp.einsum(
        "argu,gard->uad", glob_dscore, glob_query, preferred_element_type=jnp.float32
    )
    value_grad_here = jnp.einsum(
        "argu,gard->uad", glob_round, glob_grad, preferred_element_type=jnp.float32
    )
    empty_block = jnp.zeros((1, BLOCK, 2 * key_width), jnp.float32)
    spread = jnp.concatenate([window_grads[:, 0], empty_block, empty_block], axis=0)
    spread = spread + jnp.concatenate([empty_block, window_grads[:, 1], empty_block], axis=0)
    spread = spread + jnp.concatenate([empty_block, empty_block, window_grads[:, 2]], axis=0)
    rims = jnp.concatenate([spread[0], spread[-1]], axis=0)
    arrived = with_halo(rims, (("ctx", 0),), BLOCK)
    pair_grad = spread[1:-1].reshape(tok_rows, 2 * key_width)
    pair_grad = pair_grad.at[:BLOCK].add(arrived[:BLOCK])
    pair_grad = pair_grad.at[tok_rows - BLOCK :].add(arrived[3 * BLOCK :])
    pair_grad = pair_grad + jnp.concatenate(
        [key_grad_here.reshape(tok_rows, key_width), value_grad_here.reshape(tok_rows, key_width)],
        axis=1,
    )
    glob_grads = jnp.concatenate(
        [glob_query_grad.reshape(glob_count, query_width), glob_key_grad, glob_value_grad], axis=1
    )
    laid = (
        jnp.zeros((ctx_count * CAP, glob_grads.shape[1]), jnp.float32).at[slot_of].set(glob_grads)
    )
    returned = lax.psum_scatter(laid, "ctx", scatter_dimension=0, tiled=True)
    target = jnp.where(slot_ok, slot_row, tok_rows)
    grad_query_all = grad_query_loc.at[target].add(returned[:, :query_width], mode="drop")
    pair_grad = pair_grad.at[target].add(returned[:, query_width:], mode="drop")
    glob_rows_out = jnp.transpose(glob_attended, (2, 0, 1, 3)).reshape(glob_count, query_width)
    attended_all = attended_loc.at[jnp.where(is_mine, safe_row, tok_rows)].set(
        glob_rows_out, mode="drop"
    )
    return (
        attended_all.astype(jnp.bfloat16),
        grad_query_all.astype(jnp.bfloat16),
        pair_grad[:, :key_width].astype(jnp.bfloat16),
        pair_grad[:, key_width:].astype(jnp.bfloat16),
    )


MESH = pl.DeviceIdType.MESH
ROWS = 4
REP = HQ // HK
TOK = 128
FAR = -1e30


def dense_kernel(
    pos_row, q_in, k_in, v_in, g_in,
    att_out, gq_out, gk_ref, gv_ref,
    q_ref, g_ref, att_ref, gq_ref,
    kv, qt, gt, qs, gs, sbuf, dbuf, pbuf, wbuf, top8, total8, mixed8,
    acc, xsend, xrecv, csend, crecv, erecv,
    in_s, out_s, ax_s, ax_r, au_s, au_r, ad_s, ad_r, ek_s, ek_r, rx_s, rx_r, rc_s, rc_r, ex_s, ex_r,
):
    c = lax.axis_index("ctx")
    z, x = c // 2, c % 2
    partner = c + 1 - 2 * x
    scale = 1.0 / math.sqrt(DH)
    half = HK // 2 * DH
    wide = REP * TOK

    def rows(block):
        return pl.ds(pl.multiple_of(block * TOK, TOK), TOK)

    def head(j):
        return pl.ds(pl.multiple_of(j * DH, DH), DH)

    loads = [
        pltpu.make_async_copy(source, target, in_s.at[i])
        for i, (source, target) in enumerate(
            [
                (source.at[:, pl.ds(h * half, half)], kv.at[h, rows(c), pl.ds(i * half, half)])
                for h in (0, 1)
                for i, source in enumerate((k_in, v_in))
            ]
            + [(q_in, q_ref), (g_in, g_ref)]
        )
    ]
    for load in loads:
        load.start()

    barrier = pltpu.get_barrier_semaphore()
    pl.semaphore_signal(barrier, inc=1, device_id={"ctx": partner}, device_id_type=MESH)

    @pl.when(z > 0)
    def _():
        pl.semaphore_signal(barrier, inc=1, device_id={"ctx": c - 2}, device_id_type=MESH)

    @pl.when(z < ROWS - 1)
    def _():
        pl.semaphore_signal(barrier, inc=1, device_id={"ctx": c + 2}, device_id_type=MESH)

    pl.semaphore_wait(
        barrier, 1 + (z > 0).astype(jnp.int32) + (z < ROWS - 1).astype(jnp.int32)
    )

    def remote(source, target, send, recv, device):
        return pltpu.make_async_remote_copy(
            src_ref=source, dst_ref=target, send_sem=send, recv_sem=recv,
            device_id={"ctx": device}, device_id_type=MESH,
        )

    def along(h, k, up):
        block = c - 2 * (k - 1) if up else c + 2 * (k - 1)
        here = kv.at[h, rows(block)]
        send, recv = (au_s, au_r) if up else (ad_s, ad_r)
        return remote(
            here, here,
            send.at[h, k - 1], recv.at[h, k - 1], c + 2 if up else c - 2,
        )

    def along_in(h, k, up):
        block = c - 2 * k if up else c + 2 * k
        here = kv.at[h, rows(block)]
        send, recv = (au_s, au_r) if up else (ad_s, ad_r)
        return remote(here, here, send.at[h, k - 1], recv.at[h, k - 1], partner)

    def across(h, zz):
        here = kv.at[h, rows(2 * zz + x)]
        return remote(here, here, ax_s.at[h, zz], ax_r.at[h, zz], partner)

    def across_in(h, zz):
        here = kv.at[h, rows(2 * zz + 1 - x)]
        return remote(here, here, ax_s.at[h, zz], ax_r.at[h, zz], partner)

    def send_own(h):
        loads[2 * h].wait()
        loads[2 * h + 1].wait()
        across(h, z).start()

        @pl.when(z < ROWS - 1)
        def _():
            along(h, 1, True).start()

        @pl.when(z > 0)
        def _():
            along(h, 1, False).start()

    send_own(0)

    def beside(up):
        here = kv.at[0, rows(2 * z + 1 - x)]
        i = 0 if up else 1
        return remote(here, here, ek_s.at[i], ek_r.at[i], c + 2 if up else c - 2)

    def beside_in(up):
        here = kv.at[0, rows(2 * (z - 1 if up else z + 1) + 1 - x)]
        i = 0 if up else 1
        return remote(here, here, ek_s.at[i], ek_r.at[i], partner)

    for load in loads[4:]:
        load.wait()

    def stack(j, carry):
        for r in range(REP):
            cols = pl.ds(pl.multiple_of((j * REP + r) * DH, DH), DH)
            part = q_ref[:, cols]
            qs[j, r * TOK : (r + 1) * TOK, :] = part
            qt[j, :, r * TOK : (r + 1) * TOK] = part.astype(jnp.float32).T.astype(jnp.bfloat16)
            part = g_ref[:, cols]
            gs[j, r * TOK : (r + 1) * TOK, :] = part
            gt[j, :, r * TOK : (r + 1) * TOK] = part.astype(jnp.float32).T.astype(jnp.bfloat16)
        return carry

    lax.fori_loop(0, HK, stack, 0)
    top8[...] = jnp.full(top8.shape, FAR, jnp.float32)
    total8[...] = jnp.zeros(total8.shape, jnp.float32)
    mixed8[...] = jnp.zeros(mixed8.shape, jnp.float32)

    glob_count = pos_row.shape[1]

    def is_glob(block):
        token = block * TOK + lax.broadcasted_iota(jnp.int32, (TOK, glob_count), 0)
        return jnp.max(jnp.where(pos_row[...] == token, 1.0, 0.0), axis=1, keepdims=True)

    row_glob = jnp.broadcast_to(is_glob(c), (TOK, TOK)).T

    def block_bias(block):
        col_glob = is_glob(block)
        u_block = block * (TOK // BLOCK) + lax.broadcasted_iota(jnp.int32, (TOK, TOK), 0) // BLOCK
        t_block = c * (TOK // BLOCK) + lax.broadcasted_iota(jnp.int32, (TOK, TOK), 1) // BLOCK
        near = jnp.where(jnp.abs(u_block - t_block) <= 1, 1.0, 0.0)
        allowed = jnp.maximum(jnp.maximum(near, row_glob), col_glob)
        bias = jnp.where(allowed > 0.5, 0.0, FAR)
        return jnp.concatenate([bias] * REP, axis=1)

    def scores(h, block):
        bias = block_bias(block)
        at = rows(block)

        def one(i, carry):
            j = 2 * h + i
            s = jnp.dot(kv[h, at, head(i)], qt[j], preferred_element_type=jnp.float32)
            s = s * scale + bias
            sbuf[j, at, :] = s
            d = jnp.dot(
                kv[h, at, head(i + HK // 2)], gt[j], preferred_element_type=jnp.float32
            )
            dbuf[j, at, :] = d
            s = s.reshape(TOK // 8, 8, wide)
            old = top8[j]
            new = jnp.maximum(old, jnp.max(s, axis=0))
            factor = jnp.exp(old - new)
            e = jnp.exp(s - new[None])
            top8[j] = new
            total8[j] = total8[j] * factor + jnp.sum(e, axis=0)
            e = e * d.reshape(TOK // 8, 8, wide)
            mixed8[j] = mixed8[j] * factor + jnp.sum(e, axis=0)
            return carry

        lax.fori_loop(0, HK // 2, one, 0)

    edge = (z == 0) | (z == ROWS - 1)
    two = jnp.where(z >= 2, z - 2, z + 2)

    def forward(h, k):
        @pl.when(z - k >= 0)
        def _():
            along_in(h, k, True).wait_recv()

            if k < ROWS - 1:

                @pl.when(z < ROWS - 1)
                def _():
                    along(h, k + 1, True).start()

            if h == 1 or k > 1:
                across(h, z - k).start()

        @pl.when(z + k < ROWS)
        def _():
            along_in(h, k, False).wait_recv()

            if k < ROWS - 1:

                @pl.when(z > 0)
                def _():
                    along(h, k + 1, False).start()

            if h == 1 or k > 1:
                across(h, z + k).start()

    def scores_next(h, other):
        @pl.when(z > 0)
        def _():
            if other:
                (beside_in(True) if h == 0 else across_in(1, z - 1)).wait_recv()
            scores(h, 2 * (z - 1) + (1 - x if other else x))

        @pl.when(z < ROWS - 1)
        def _():
            if other:
                (beside_in(False) if h == 0 else across_in(1, z + 1)).wait_recv()
            scores(h, 2 * (z + 1) + (1 - x if other else x))

    def scores_far(h, k, other):
        zz = two if k == 2 else ROWS - 1 - z

        def go():
            if other:
                across_in(h, zz).wait_recv()
            scores(h, 2 * zz + (1 - x if other else x))

        if k == 2:
            go()
        else:
            pl.when(edge)(go)

    def stats(h):
        for j in (2 * h, 2 * h + 1):
            top = jnp.max(top8[j], axis=0, keepdims=True)
            factor = jnp.exp(top8[j] - top)
            reciprocal = 1.0 / jnp.sum(total8[j] * factor, axis=0, keepdims=True)
            delta = jnp.sum(mixed8[j] * factor, axis=0, keepdims=True) * reciprocal
            top8[j] = jnp.broadcast_to(top, (8, wide))
            total8[j] = jnp.broadcast_to(reciprocal, (8, wide))
            mixed8[j] = jnp.broadcast_to(delta, (8, wide))

    def terms(h, block, out):
        at = rows(block)

        def one(i, carry):
            j = 2 * h + i
            p = jnp.exp(sbuf[j, at, :] - top8[j, 0:1, :]) * total8[j, 0:1, :]
            w = (p * (dbuf[j, at, :] - mixed8[j, 0:1, :])).astype(jnp.bfloat16)
            p = p.astype(jnp.bfloat16)
            pbuf[j, at, :] = p
            wbuf[j, at, :] = w
            dk = jnp.dot(w, qs[j], preferred_element_type=jnp.float32) * scale
            dv = jnp.dot(p, gs[j], preferred_element_type=jnp.float32)
            out[:, head(i)] = dk.astype(out.dtype)
            out[:, head(i + HK // 2)] = dv.astype(out.dtype)
            return carry

        lax.fori_loop(0, HK // 2, one, 0)

    def pick(a, b, d, e):
        return jnp.where(z == 0, a, jnp.where(z == 1, b, jnp.where(z == 2, d, e)))

    order = (pick(3, 3, 0, 0), pick(2, 0, 3, 1), pick(1, 2, 1, 2), z)

    def cross(h, o):
        return remote(
            xsend.at[o, h], xrecv.at[o, h], rx_s.at[h, o], rx_r.at[h, o], partner
        )

    near = (None, (z == 1) | (z == 2), None, None)

    def extra(o):
        down = order[o] < z
        i = jnp.where(down, 1, 0)
        return remote(
            xsend.at[o, 0], erecv.at[i], ex_s.at[i], ex_r.at[i], jnp.where(down, c - 2, c + 2)
        )

    def extra_in(i):
        return remote(erecv.at[i], erecv.at[i], ex_s.at[i], ex_r.at[i], partner)

    def phase(h, o):
        terms(h, 2 * order[o] + 1 - x, xsend.at[o, h])
        if h == 1 or o == 0:
            cross(h, o).start()
        elif o == 2:
            extra(2).start()
        elif o == 1:

            @pl.when(near[1])
            def _():
                extra(1).start()

            @pl.when(jnp.logical_not(near[1]))
            def _():
                cross(0, 1).start()

        else:

            @pl.when(z > 0)
            def _():
                extra_in(0).wait_recv()
                both = xsend[3, 0].astype(jnp.float32) + erecv[0].astype(jnp.float32)
                xsend[3, 0] = both.astype(jnp.bfloat16)

            @pl.when(z < ROWS - 1)
            def _():
                extra_in(1).wait_recv()
                both = xsend[3, 0].astype(jnp.float32) + erecv[1].astype(jnp.float32)
                xsend[3, 0] = both.astype(jnp.bfloat16)

            cross(0, 3).start()
        terms(h, 2 * order[o] + x, acc.at[o, h])

    def chain(h, o):
        down = order[o] < z
        to = jnp.where(down, z - 1, z + 1)
        slot = jnp.where((to == order[o]) & jnp.logical_not(down), ROWS, order[o])
        return remote(
            csend.at[o, h], crecv.at[slot, h], rc_s.at[h, o], rc_r.at[h, slot], 2 * to + x
        )

    def chain_in(h, slot):
        return remote(crecv.at[slot, h], crecv.at[slot, h], rc_s.at[h, 0], rc_r.at[h, slot], partner)

    def pass_on(h, o):
        down = order[o] < z
        fed = (down & (z < ROWS - 1)) | (jnp.logical_not(down) & (z > 0))

        def add_crossed():
            cross(h, o).wait_recv()
            acc[o, h] = acc[o, h] + xrecv[o, h].astype(jnp.float32)

        if h == 1 or o == 0:
            add_crossed()
        elif o == 1:
            pl.when(jnp.logical_not(near[1]))(add_crossed)

        @pl.when(fed)
        def _():
            chain_in(h, order[o]).wait_recv()
            acc[o, h] = acc[o, h] + crecv[order[o], h].astype(jnp.float32)

        csend[o, h] = acc[o, h].astype(jnp.bfloat16)
        chain(h, o).start()

    def outputs(h):
        def one(i, carry):
            j = 2 * h + i
            over_keys = (((0,), (0,)), ((), ()))
            mixed = lax.dot_general(
                kv[h, :, head(i + HK // 2)], pbuf[j], over_keys,
                preferred_element_type=jnp.float32,
            )
            grad = scale * lax.dot_general(
                kv[h, :, head(i)], wbuf[j], over_keys, preferred_element_type=jnp.float32
            )
            for r in range(REP):
                cols = pl.ds(pl.multiple_of((j * REP + r) * DH, DH), DH)
                att_ref[:, cols] = mixed[:, r * TOK : (r + 1) * TOK].T.astype(jnp.bfloat16)
                gq_ref[:, cols] = grad[:, r * TOK : (r + 1) * TOK].T.astype(jnp.bfloat16)
            return carry

        lax.fori_loop(0, HK // 2, one, 0)

    def finish(h):
        last = ROWS - 1
        cross(h, last).wait_recv()
        acc[last, h] = acc[last, h] + xrecv[last, h].astype(jnp.float32)

        @pl.when(z < ROWS - 1)
        def _():
            chain_in(h, z).wait_recv()
            acc[last, h] = acc[last, h] + crecv[z, h].astype(jnp.float32)

        @pl.when(z > 0)
        def _():
            chain_in(h, ROWS).wait_recv()
            acc[last, h] = acc[last, h] + crecv[ROWS, h].astype(jnp.float32)

        gk_ref[:, h * half : (h + 1) * half] = acc[last, h, :, :half].astype(jnp.bfloat16)
        gv_ref[:, h * half : (h + 1) * half] = acc[last, h, :, half:].astype(jnp.bfloat16)

    scores(0, c)
    forward(0, 1)
    send_own(1)
    across_in(0, z).wait_recv()

    @pl.when(z < ROWS - 1)
    def _():
        beside(True).start()

    @pl.when(z > 0)
    def _():
        beside(False).start()

    scores_next(0, False)
    forward(0, 2)
    scores(0, 2 * z + 1 - x)
    forward(1, 1)
    scores_far(0, 2, False)
    forward(0, 3)
    scores_next(0, True)
    forward(1, 2)
    scores_far(0, 3, False)
    scores_far(0, 2, True)
    scores_far(0, 3, True)
    stats(0)
    phase(0, 0)
    forward(1, 3)
    scores(1, c)
    across_in(1, z).wait_recv()
    scores(1, 2 * z + 1 - x)
    phase(0, 1)
    scores_next(1, False)
    phase(0, 2)

    @pl.when(edge)
    def _():
        pass_on(0, 2)

    pass_on(0, 0)
    scores_far(1, 2, False)
    scores_next(1, True)
    phase(0, 3)
    scores_far(1, 3, False)
    scores_far(1, 2, True)
    scores_far(1, 3, True)
    stats(1)
    phase(1, 0)
    pass_on(0, 1)
    phase(1, 1)

    @pl.when(jnp.logical_not(edge))
    def _():
        pass_on(0, 2)

    phase(1, 2)
    pass_on(1, 0)
    phase(1, 3)
    finish(0)
    outputs(0)
    pass_on(1, 1)
    outputs(1)
    stores = [
        pltpu.make_async_copy(att_ref, att_out, out_s.at[0]),
        pltpu.make_async_copy(gq_ref, gq_out, out_s.at[1]),
    ]
    for store in stores:
        store.start()
    pass_on(1, 2)
    finish(1)

    for store in stores:
        store.wait()
    across(0, z).wait_send()
    for h in (0, 1):
        cross(h, 0).wait_send()
        cross(h, 3).wait_send()
    cross(1, 1).wait_send()
    cross(1, 2).wait_send()
    extra(2).wait_send()

    @pl.when(near[1])
    def _():
        extra(1).wait_send()

    @pl.when(jnp.logical_not(near[1]))
    def _():
        cross(0, 1).wait_send()

    @pl.when(z < ROWS - 1)
    def _():
        beside(True).wait_send()

    @pl.when(z > 0)
    def _():
        beside(False).wait_send()

    for zz in range(ROWS):
        across(1, zz).wait_send()

        @pl.when(jnp.abs(z - zz) > 1)
        def _():
            across(0, zz).wait_send()

    for h in (0, 1):
        for o in range(ROWS - 1):
            chain(h, o).wait_send()
        for k in range(1, ROWS):

            @pl.when((z - (k - 1) >= 0) & (z < ROWS - 1))
            def _():
                along(h, k, True).wait_send()

            @pl.when((z + (k - 1) < ROWS) & (z > 0))
            def _():
                along(h, k, False).wait_send()


def copy_kernel(*refs):
    count = 4
    ins, outs, held = (refs[i * count : (i + 1) * count] for i in range(3))
    sems = refs[3 * count]
    loads = [pltpu.make_async_copy(ins[i], held[i], sems.at[0, i]) for i in range(count)]
    stores = [pltpu.make_async_copy(held[i], outs[i], sems.at[1, i]) for i in range(count)]
    for load in loads:
        load.start()
    for load, store in zip(loads, stores):
        load.wait()
        store.start()
    for store in stores:
        store.wait()


def dense(queries, keys, values, grad_out, positions):
    tokens = TOK * 2 * ROWS
    key_width = HK * DH
    wide = REP * TOK
    bf16, f32 = jnp.bfloat16, jnp.float32
    vmem = pl.BlockSpec(memory_space=pltpu.VMEM)
    dma = pltpu.SemaphoreType.DMA
    anywhere = pl.BlockSpec(memory_space=pl.ANY)
    shapes = [
        jax.ShapeDtypeStruct((TOK, HQ * DH), bf16),
        jax.ShapeDtypeStruct((TOK, HQ * DH), bf16),
        jax.ShapeDtypeStruct((TOK, key_width), bf16),
        jax.ShapeDtypeStruct((TOK, key_width), bf16),
    ]
    results = pl.pallas_call(
        dense_kernel,
        out_shape=shapes,
        in_specs=[vmem] + [anywhere] * 4,
        out_specs=[anywhere] * 2 + [vmem] * 2,
        scratch_shapes=[
            pltpu.VMEM((TOK, HQ * DH), bf16),
            pltpu.VMEM((TOK, HQ * DH), bf16),
            pltpu.VMEM((TOK, HQ * DH), bf16),
            pltpu.VMEM((TOK, HQ * DH), bf16),
            pltpu.VMEM((2, tokens, key_width), bf16),
            pltpu.VMEM((HK, DH, wide), bf16),
            pltpu.VMEM((HK, DH, wide), bf16),
            pltpu.VMEM((HK, wide, DH), bf16),
            pltpu.VMEM((HK, wide, DH), bf16),
            pltpu.VMEM((HK, tokens, wide), f32),
            pltpu.VMEM((HK, tokens, wide), f32),
            pltpu.VMEM((HK, tokens, wide), bf16),
            pltpu.VMEM((HK, tokens, wide), bf16),
            pltpu.VMEM((HK, 8, wide), f32),
            pltpu.VMEM((HK, 8, wide), f32),
            pltpu.VMEM((HK, 8, wide), f32),
            pltpu.VMEM((ROWS, 2, TOK, key_width), f32),
            pltpu.VMEM((ROWS, 2, TOK, key_width), bf16),
            pltpu.VMEM((ROWS, 2, TOK, key_width), bf16),
            pltpu.VMEM((ROWS - 1, 2, TOK, key_width), bf16),
            pltpu.VMEM((ROWS + 1, 2, TOK, key_width), bf16),
            pltpu.VMEM((2, TOK, key_width), bf16),
            dma((6,)),
            dma((2,)),
            dma((2, ROWS)),
            dma((2, ROWS)),
            dma((2, ROWS - 1)),
            dma((2, ROWS - 1)),
            dma((2, ROWS - 1)),
            dma((2, ROWS - 1)),
            dma((2,)),
            dma((2,)),
            dma((2, ROWS)),
            dma((2, ROWS)),
            dma((2, ROWS - 1)),
            dma((2, ROWS + 1)),
            dma((2,)),
            dma((2,)),
        ],
        compiler_params=pltpu.CompilerParams(
            collective_id=0, has_side_effects=True, vmem_limit_bytes=56 * 1024 * 1024
        ),
    )(positions.reshape(1, -1), queries, keys, values, grad_out)
    return pl.pallas_call(
        copy_kernel,
        out_shape=shapes,
        in_specs=[anywhere] * 4,
        out_specs=[anywhere] * 4,
        scratch_shapes=[pltpu.VMEM(a.shape, bf16) for a in shapes] + [dma((2, 4))],
    )(*results)


def choose(queries, keys, values, grad_out, positions):
    if lax.axis_size("ctx") == 2 * ROWS and queries.shape[0] == TOK:
        return tuple(dense(queries, keys, values, grad_out, positions))
    return local(queries, keys, values, grad_out, positions)


def solution(mesh):
    in_specs = (
        P(("dp", "ctx"), None),
        P(("dp", "ctx"), None),
        P(("dp", "ctx"), None),
        P(("dp", "ctx"), None),
        P("dp"),
    )
    out_specs = (
        P(("dp", "ctx"), None),
        P(("dp", "ctx"), None),
        P(("dp", "ctx"), None),
        P(("dp", "ctx"), None),
    )
    return jax.shard_map(choose, mesh=mesh, in_specs=in_specs, out_specs=out_specs, check_vma=False)
```

```python
import functools
import math

import jax
import jax.numpy as jnp
from jax import lax
from jax.experimental import pallas as pl
from jax.experimental.pallas import tpu as pltpu
from jax.sharding import PartitionSpec as P

HQ = 16
HK = 4
DH = 128
BLOCK = 64
CAP = 32


highest = lax.Precision.HIGHEST


def with_halo(array, sides, width):
    for axis, dim in sides:
        size, length = (lax.axis_size(axis), array.shape[dim])
        up = [(i, (i + 1) % size) for i in range(size - 1)]
        down = [(j, i) for i, j in up]
        last = lax.slice_in_dim(array, length - width, length, axis=dim)
        first = lax.slice_in_dim(array, 0, width, axis=dim)
        before = lax.ppermute(last, axis, up)
        after = lax.ppermute(first, axis, down)
        array = jnp.concatenate([before, array, after], axis=dim)
    return array


def combined_all(part, axis, combine):
    gathered = jax.tree.map(lambda a: lax.all_gather(a, axis), part)

    def take(source):
        return jax.tree.map(lambda a: lax.dynamic_index_in_dim(a, source, 0, False), gathered)

    return lax.fori_loop(
        1, lax.axis_size(axis), lambda source, state: combine(state, take(source)), take(0)
    )


def window_group(pieces, glob_keys, glob_values, score_scale):
    query_block, grad_block, key_window, value_window, key_usable, query_live = pieces
    near = (
        jnp.einsum("bqard,bkad->barqk", query_block, key_window, preferred_element_type=jnp.float32)
        * score_scale
    )
    far = (
        jnp.einsum("bqard,gad->barqg", query_block, glob_keys, preferred_element_type=jnp.float32)
        * score_scale
    )
    near = jnp.where(key_usable[:, None, None, None, :], near, -jnp.inf)
    row_top = jnp.maximum(jnp.max(near, axis=-1), jnp.max(far, axis=-1))
    near_weight = jnp.exp(near - row_top[..., None])
    far_weight = jnp.exp(far - row_top[..., None])
    total = jnp.sum(near_weight, axis=-1) + jnp.sum(far_weight, axis=-1)
    mixed = jnp.einsum(
        "barqk,bkad->bqard",
        near_weight.astype(jnp.bfloat16),
        value_window,
        preferred_element_type=jnp.float32,
    )
    mixed = mixed + jnp.einsum(
        "barqg,gad->bqard",
        far_weight.astype(jnp.bfloat16),
        glob_values,
        preferred_element_type=jnp.float32,
    )
    attended = mixed / jnp.transpose(total, (0, 3, 1, 2))[..., None]
    delta = jnp.transpose(jnp.sum(grad_block * attended, axis=-1), (0, 2, 3, 1))
    live = query_live[:, None, None, :, None]
    near_prob = near_weight / total[..., None]
    far_prob = far_weight / total[..., None]
    near_dprob = jnp.einsum(
        "bqard,bkad->barqk", grad_block, value_window, preferred_element_type=jnp.float32
    )
    far_dprob = jnp.einsum(
        "bqard,gad->barqg", grad_block, glob_values, preferred_element_type=jnp.float32
    )
    near_dscore = (near_prob * (near_dprob - delta[..., None]) * live).astype(jnp.bfloat16)
    far_dscore = (far_prob * (far_dprob - delta[..., None]) * live).astype(jnp.bfloat16)
    near_round = (near_prob * live).astype(jnp.bfloat16)
    far_round = (far_prob * live).astype(jnp.bfloat16)
    grad_query = jnp.einsum(
        "barqk,bkad->bqard", near_dscore, key_window, preferred_element_type=jnp.float32
    )
    grad_query = score_scale * (
        grad_query
        + jnp.einsum("barqg,gad->bqard", far_dscore, glob_keys, preferred_element_type=jnp.float32)
    )
    grad_key_win = score_scale * jnp.einsum(
        "barqk,bqard->bkad", near_dscore, query_block, preferred_element_type=jnp.float32
    )
    grad_value_win = jnp.einsum(
        "barqk,bqard->bkad", near_round, grad_block, preferred_element_type=jnp.float32
    )
    grad_key_glob = score_scale * jnp.einsum(
        "barqg,bqard->gad", far_dscore, query_block, preferred_element_type=jnp.float32
    )
    grad_value_glob = jnp.einsum(
        "barqg,bqard->gad", far_round, grad_block, preferred_element_type=jnp.float32
    )
    return (attended, grad_query, grad_key_win, grad_value_win, grad_key_glob, grad_value_glob)


def combine_softmax(left_part, right_part):
    left_top, left_total, left_summed = left_part
    right_top, right_total, right_summed = right_part
    joint_top = jnp.maximum(left_top, right_top)
    left_factor = jnp.exp(left_top - joint_top)
    right_factor = jnp.exp(right_top - joint_top)
    return (
        joint_top,
        left_total * left_factor + right_total * right_factor,
        left_summed * left_factor[..., None] + right_summed * right_factor[..., None],
    )


def local(queries, keys, values, grad_out, positions):
    tok_rows = queries.shape[0]
    query_width = queries.shape[1]
    key_width = keys.shape[1]
    q_per_kv = HQ // HK
    ctx_count = lax.axis_size("ctx")
    seq_total = tok_rows * ctx_count
    first_row = lax.axis_index("ctx") * tok_rows
    score_scale = 1.0 / math.sqrt(DH)
    glob_count = positions.shape[0]
    local_row = positions - first_row
    is_mine = (local_row >= 0) & (local_row < tok_rows)
    safe_row = jnp.clip(local_row, 0, tok_rows - 1)
    before = jnp.sum((positions < first_row).astype(jnp.int32))
    held_count = jnp.sum(is_mine.astype(jnp.int32))
    slot_index = jnp.arange(CAP)
    slot_ok = slot_index < held_count
    slot_row = jnp.clip(
        positions[jnp.clip(before + slot_index, 0, glob_count - 1)] - first_row, 0, tok_rows - 1
    )
    owner_index = positions // tok_rows
    owner_start = jnp.sum((owner_index[None, :] < owner_index[:, None]).astype(jnp.int32), axis=1)
    slot_of = owner_index * CAP + jnp.arange(glob_count) - owner_start
    packed = jnp.concatenate(
        [queries[slot_row], keys[slot_row], values[slot_row], grad_out[slot_row]], axis=1
    )
    packed = jnp.where(slot_ok[:, None], packed, jnp.zeros_like(packed))
    everyone = lax.all_gather(packed, "ctx", axis=0, tiled=True)
    compact = everyone[slot_of]
    glob_query = compact[:, :query_width].reshape(glob_count, HK, q_per_kv, DH)
    glob_keys = compact[:, query_width : query_width + key_width].reshape(glob_count, HK, DH)
    glob_values = compact[:, query_width + key_width : query_width + 2 * key_width].reshape(
        glob_count, HK, DH
    )
    glob_grad = compact[:, query_width + 2 * key_width :].reshape(glob_count, HK, q_per_kv, DH)
    paired = jnp.concatenate([keys, values], axis=1)
    extended = with_halo(paired, (("ctx", 0),), BLOCK)
    blocks = tok_rows // BLOCK
    ext_blocks = extended.reshape(blocks + 2, BLOCK, 2 * key_width)
    window = jnp.concatenate([ext_blocks[:-2], ext_blocks[1:-1], ext_blocks[2:]], axis=1)
    key_window = window[:, :, :key_width].reshape(blocks, 3 * BLOCK, HK, DH)
    value_window = window[:, :, key_width:].reshape(blocks, 3 * BLOCK, HK, DH)
    ext_position = first_row - BLOCK + jnp.arange(tok_rows + 2 * BLOCK)
    ext_global = jnp.any(ext_position[:, None] == positions[None, :], axis=1)
    ext_usable = (
        (ext_position >= 0) & (ext_position < seq_total) & jnp.logical_not(ext_global)
    ).reshape(blocks + 2, BLOCK)
    key_usable = jnp.concatenate([ext_usable[:-2], ext_usable[1:-1], ext_usable[2:]], axis=1)
    query_live = (
        jnp.logical_not(ext_global[BLOCK : BLOCK + tok_rows])
        .astype(jnp.float32)
        .reshape(blocks, BLOCK)
    )
    per_step = min(8, blocks)
    step_count = blocks // per_step

    def regroup(source):
        return source.reshape((step_count, per_step) + source.shape[1:])

    stacked = (
        regroup(queries.reshape(blocks, BLOCK, HK, q_per_kv, DH)),
        regroup(grad_out.reshape(blocks, BLOCK, HK, q_per_kv, DH)),
        regroup(key_window),
        regroup(value_window),
        regroup(key_usable),
        regroup(query_live),
    )
    results = lax.map(
        lambda pieces: window_group(pieces, glob_keys, glob_values, score_scale), stacked
    )
    attended_loc = results[0].reshape(tok_rows, query_width)
    grad_query_loc = results[1].reshape(tok_rows, query_width)
    window_grads = jnp.concatenate(
        [
            results[2].reshape(blocks, 3, BLOCK, key_width),
            results[3].reshape(blocks, 3, BLOCK, key_width),
        ],
        axis=3,
    )
    glob_key_grad = jnp.sum(results[4], axis=0).reshape(glob_count, key_width)
    glob_value_grad = jnp.sum(results[5], axis=0).reshape(glob_count, key_width)
    key_here = keys.reshape(tok_rows, HK, DH)
    value_here = values.reshape(tok_rows, HK, DH)
    glob_score = (
        jnp.einsum("gard,uad->argu", glob_query, key_here, preferred_element_type=jnp.float32)
        * score_scale
    )
    top_here = jnp.max(glob_score, axis=-1)
    weight_here = jnp.exp(glob_score - top_here[..., None])
    total_here = jnp.sum(weight_here, axis=-1)
    summed_here = jnp.einsum(
        "argu,uad->argd", weight_here, value_here.astype(jnp.float32), precision=highest
    )
    glob_top, glob_total, glob_summed = combined_all(
        (top_here, total_here, summed_here), "ctx", combine_softmax
    )
    glob_attended = glob_summed / glob_total[..., None]
    glob_delta = jnp.sum(
        jnp.transpose(glob_grad, (1, 2, 0, 3)).astype(jnp.float32) * glob_attended, axis=-1
    )
    glob_prob = jnp.exp(glob_score - glob_top[..., None]) / glob_total[..., None]
    glob_dprob = jnp.einsum(
        "gard,uad->argu", glob_grad, value_here, preferred_element_type=jnp.float32
    )
    glob_dscore = (glob_prob * (glob_dprob - glob_delta[..., None])).astype(jnp.bfloat16)
    glob_round = glob_prob.astype(jnp.bfloat16)
    glob_query_grad = score_scale * jnp.einsum(
        "argu,uad->gard", glob_dscore, key_here, preferred_element_type=jnp.float32
    )
    key_grad_here = score_scale * jnp.einsum(
        "argu,gard->uad", glob_dscore, glob_query, preferred_element_type=jnp.float32
    )
    value_grad_here = jnp.einsum(
        "argu,gard->uad", glob_round, glob_grad, preferred_element_type=jnp.float32
    )
    empty_block = jnp.zeros((1, BLOCK, 2 * key_width), jnp.float32)
    spread = jnp.concatenate([window_grads[:, 0], empty_block, empty_block], axis=0)
    spread = spread + jnp.concatenate([empty_block, window_grads[:, 1], empty_block], axis=0)
    spread = spread + jnp.concatenate([empty_block, empty_block, window_grads[:, 2]], axis=0)
    rims = jnp.concatenate([spread[0], spread[-1]], axis=0)
    arrived = with_halo(rims, (("ctx", 0),), BLOCK)
    pair_grad = spread[1:-1].reshape(tok_rows, 2 * key_width)
    pair_grad = pair_grad.at[:BLOCK].add(arrived[:BLOCK])
    pair_grad = pair_grad.at[tok_rows - BLOCK :].add(arrived[3 * BLOCK :])
    pair_grad = pair_grad + jnp.concatenate(
        [key_grad_here.reshape(tok_rows, key_width), value_grad_here.reshape(tok_rows, key_width)],
        axis=1,
    )
    glob_grads = jnp.concatenate(
        [glob_query_grad.reshape(glob_count, query_width), glob_key_grad, glob_value_grad], axis=1
    )
    laid = (
        jnp.zeros((ctx_count * CAP, glob_grads.shape[1]), jnp.float32).at[slot_of].set(glob_grads)
    )
    returned = lax.psum_scatter(laid, "ctx", scatter_dimension=0, tiled=True)
    target = jnp.where(slot_ok, slot_row, tok_rows)
    grad_query_all = grad_query_loc.at[target].add(returned[:, :query_width], mode="drop")
    pair_grad = pair_grad.at[target].add(returned[:, query_width:], mode="drop")
    glob_rows_out = jnp.transpose(glob_attended, (2, 0, 1, 3)).reshape(glob_count, query_width)
    attended_all = attended_loc.at[jnp.where(is_mine, safe_row, tok_rows)].set(
        glob_rows_out, mode="drop"
    )
    return (
        attended_all.astype(jnp.bfloat16),
        grad_query_all.astype(jnp.bfloat16),
        pair_grad[:, :key_width].astype(jnp.bfloat16),
        pair_grad[:, key_width:].astype(jnp.bfloat16),
    )


MESH = pl.DeviceIdType.MESH
ROWS = 4
REP = HQ // HK
TOK = 128
FAR = -1e30


def dense_kernel(
    pos_row, q_in, k_in, v_in, g_in,
    att_out, gq_out, gk_ref, gv_ref,
    q_ref, g_ref, att_ref, gq_ref,
    kbuf, vbuf, qt, gt, qs, gs, sbuf, dbuf, pbuf, wbuf, top8, total8, mixed8,
    acc, xsend, xrecv, csend, crecv,
    in_s, out_s, ax_s, ax_r, au_s, au_r, ad_s, ad_r, rx_s, rx_r, rc_s, rc_r,
):
    c = lax.axis_index("ctx")
    z, x = c // 2, c % 2
    partner = c + 1 - 2 * x
    scale = 1.0 / math.sqrt(DH)
    own = (k_in, v_in)
    bufs = (kbuf, vbuf)
    wide = REP * TOK

    def rows(block):
        return pl.ds(pl.multiple_of(block * TOK, TOK), TOK)

    def head(j):
        return pl.ds(pl.multiple_of(j * DH, DH), DH)

    loads = [
        pltpu.make_async_copy(source, target, in_s.at[i])
        for i, (source, target) in enumerate(
            ((k_in, kbuf.at[rows(c)]), (v_in, vbuf.at[rows(c)]), (q_in, q_ref), (g_in, g_ref))
        )
    ]
    for load in loads:
        load.start()

    barrier = pltpu.get_barrier_semaphore()
    pl.semaphore_signal(barrier, inc=1, device_id={"ctx": partner}, device_id_type=MESH)

    @pl.when(z > 0)
    def _():
        pl.semaphore_signal(barrier, inc=1, device_id={"ctx": c - 2}, device_id_type=MESH)

    @pl.when(z < ROWS - 1)
    def _():
        pl.semaphore_signal(barrier, inc=1, device_id={"ctx": c + 2}, device_id_type=MESH)

    pl.semaphore_wait(
        barrier, 1 + (z > 0).astype(jnp.int32) + (z < ROWS - 1).astype(jnp.int32)
    )

    def remote(source, target, send, recv, device):
        return pltpu.make_async_remote_copy(
            src_ref=source, dst_ref=target, send_sem=send, recv_sem=recv,
            device_id={"ctx": device}, device_id_type=MESH,
        )

    def along(h, k, up, source=None):
        block = c - 2 * (k - 1) if up else c + 2 * (k - 1)
        here = bufs[h].at[rows(block)]
        send, recv = (au_s, au_r) if up else (ad_s, ad_r)
        return remote(
            here if source is None else source, here,
            send.at[h, k - 1], recv.at[h, k - 1], c + 2 if up else c - 2,
        )

    def along_in(h, k, up):
        block = c - 2 * k if up else c + 2 * k
        here = bufs[h].at[rows(block)]
        send, recv = (au_s, au_r) if up else (ad_s, ad_r)
        return remote(here, here, send.at[h, k - 1], recv.at[h, k - 1], partner)

    def across(h, zz, source=None):
        here = bufs[h].at[rows(2 * zz + x)]
        return remote(
            here if source is None else source, here, ax_s.at[h, zz], ax_r.at[h, zz], partner
        )

    def across_in(h, zz):
        here = bufs[h].at[rows(2 * zz + 1 - x)]
        return remote(here, here, ax_s.at[h, zz], ax_r.at[h, zz], partner)

    for h in (0, 1):
        across(h, z, own[h]).start()

        @pl.when(z < ROWS - 1)
        def _():
            along(h, 1, True, own[h]).start()

        @pl.when(z > 0)
        def _():
            along(h, 1, False, own[h]).start()

    for load in loads:
        load.wait()

    def stack(j, carry):
        for r in range(REP):
            cols = pl.ds(pl.multiple_of((j * REP + r) * DH, DH), DH)
            part = q_ref[:, cols]
            qs[j, r * TOK : (r + 1) * TOK, :] = part
            qt[j, :, r * TOK : (r + 1) * TOK] = part.astype(jnp.float32).T.astype(jnp.bfloat16)
            part = g_ref[:, cols]
            gs[j, r * TOK : (r + 1) * TOK, :] = part
            gt[j, :, r * TOK : (r + 1) * TOK] = part.astype(jnp.float32).T.astype(jnp.bfloat16)
        return carry

    lax.fori_loop(0, HK, stack, 0)
    top8[...] = jnp.full(top8.shape, FAR, jnp.float32)
    total8[...] = jnp.zeros(total8.shape, jnp.float32)
    mixed8[...] = jnp.zeros(mixed8.shape, jnp.float32)

    glob_count = pos_row.shape[1]

    def is_glob(block):
        token = block * TOK + lax.broadcasted_iota(jnp.int32, (TOK, glob_count), 0)
        return jnp.max(jnp.where(pos_row[...] == token, 1.0, 0.0), axis=1, keepdims=True)

    row_glob = jnp.broadcast_to(is_glob(c), (TOK, TOK)).T

    def block_bias(block):
        col_glob = is_glob(block)
        u_block = block * (TOK // BLOCK) + lax.broadcasted_iota(jnp.int32, (TOK, TOK), 0) // BLOCK
        t_block = c * (TOK // BLOCK) + lax.broadcasted_iota(jnp.int32, (TOK, TOK), 1) // BLOCK
        near = jnp.where(jnp.abs(u_block - t_block) <= 1, 1.0, 0.0)
        allowed = jnp.maximum(jnp.maximum(near, row_glob), col_glob)
        bias = jnp.where(allowed > 0.5, 0.0, FAR)
        return jnp.concatenate([bias] * REP, axis=1)

    def scores(block):
        bias = block_bias(block)
        at = rows(block)

        def one(j, carry):
            cols = head(j)
            s = jnp.dot(kbuf[at, cols], qt[j], preferred_element_type=jnp.float32)
            s = s * scale + bias
            sbuf[j, at, :] = s
            d = jnp.dot(vbuf[at, cols], gt[j], preferred_element_type=jnp.float32)
            dbuf[j, at, :] = d
            s = s.reshape(TOK // 8, 8, wide)
            old = top8[j]
            new = jnp.maximum(old, jnp.max(s, axis=0))
            factor = jnp.exp(old - new)
            e = jnp.exp(s - new[None])
            top8[j] = new
            total8[j] = total8[j] * factor + jnp.sum(e, axis=0)
            e = e * d.reshape(TOK // 8, 8, wide)
            mixed8[j] = mixed8[j] * factor + jnp.sum(e, axis=0)
            return carry

        lax.fori_loop(0, HK, one, 0)

    scores(c)
    def gather_step(k, carry):
        @pl.when(z - k >= 0)
        def _():
            for h in (0, 1):
                along_in(h, k, True).wait_recv()

                @pl.when(z < ROWS - 1)
                def _():
                    along(h, k + 1, True).start()

                across(h, z - k).start()

        @pl.when(z + k < ROWS)
        def _():
            for h in (0, 1):
                along_in(h, k, False).wait_recv()

                @pl.when(z > 0)
                def _():
                    along(h, k + 1, False).start()

                across(h, z + k).start()

        @pl.when(z - k >= 0)
        def _():
            scores(c - 2 * k)

        @pl.when(z + k < ROWS)
        def _():
            scores(c + 2 * k)

        @pl.when(z - (k - 1) >= 0)
        def _():
            for h in (0, 1):
                across_in(h, z - (k - 1)).wait_recv()
            scores(2 * (z - (k - 1)) + 1 - x)

        @pl.when((z + (k - 1) < ROWS) & (k > 1))
        def _():
            for h in (0, 1):
                across_in(h, z + (k - 1)).wait_recv()
            scores(2 * (z + (k - 1)) + 1 - x)

        return carry

    lax.fori_loop(1, ROWS + 1, gather_step, 0)

    for j in range(HK):
        top = jnp.max(top8[j], axis=0, keepdims=True)
        factor = jnp.exp(top8[j] - top)
        reciprocal = 1.0 / jnp.sum(total8[j] * factor, axis=0, keepdims=True)
        delta = jnp.sum(mixed8[j] * factor, axis=0, keepdims=True) * reciprocal
        top8[j] = jnp.broadcast_to(top, (8, wide))
        total8[j] = jnp.broadcast_to(reciprocal, (8, wide))
        mixed8[j] = jnp.broadcast_to(delta, (8, wide))

    def terms(block, out):
        at = rows(block)

        def one(j, carry):
            cols = head(j)
            p = jnp.exp(sbuf[j, at, :] - top8[j, 0:1, :]) * total8[j, 0:1, :]
            w = (p * (dbuf[j, at, :] - mixed8[j, 0:1, :])).astype(jnp.bfloat16)
            p = p.astype(jnp.bfloat16)
            pbuf[j, at, :] = p
            wbuf[j, at, :] = w
            dk = jnp.dot(w, qs[j], preferred_element_type=jnp.float32) * scale
            dv = jnp.dot(p, gs[j], preferred_element_type=jnp.float32)
            out[0, :, cols] = dk.astype(out.dtype)
            out[1, :, cols] = dv.astype(out.dtype)
            return carry

        lax.fori_loop(0, HK, one, 0)

    def pick(a, b, d, e):
        return jnp.where(z == 0, a, jnp.where(z == 1, b, jnp.where(z == 2, d, e)))

    order = (pick(3, 3, 0, 0), pick(2, 0, 3, 1), pick(1, 2, 1, 2), z)

    def cross(h, o):
        return remote(
            xsend.at[o, h], xrecv.at[o, h], rx_s.at[h, o], rx_r.at[h, o], partner
        )

    def phase(o):
        terms(2 * order[o] + 1 - x, xsend.at[o])
        cross(0, o).start()
        cross(1, o).start()
        terms(2 * order[o] + x, acc.at[o])

    def chain(h, o):
        down = order[o] < z
        to = jnp.where(down, z - 1, z + 1)
        slot = jnp.where((to == order[o]) & jnp.logical_not(down), ROWS, order[o])
        return remote(
            csend.at[o, h], crecv.at[slot, h], rc_s.at[h, o], rc_r.at[h, slot], 2 * to + x
        )

    def chain_in(h, slot):
        return remote(crecv.at[slot, h], crecv.at[slot, h], rc_s.at[h, 0], rc_r.at[h, slot], partner)

    def pass_on(o, h):
        down = order[o] < z
        fed = (down & (z < ROWS - 1)) | (jnp.logical_not(down) & (z > 0))

        cross(h, o).wait_recv()
        acc[o, h] = acc[o, h] + xrecv[o, h].astype(jnp.float32)

        @pl.when(fed)
        def _():
            chain_in(h, order[o]).wait_recv()
            acc[o, h] = acc[o, h] + crecv[order[o], h].astype(jnp.float32)

        csend[o, h] = acc[o, h].astype(jnp.bfloat16)
        chain(h, o).start()

    phase(0)
    phase(1)
    pass_on(0, 0)
    phase(2)
    pass_on(0, 1)
    phase(3)

    def outputs(j, carry):
        across_rows = (((0,), (0,)), ((), ()))
        mixed = lax.dot_general(
            vbuf[:, head(j)], pbuf[j], across_rows, preferred_element_type=jnp.float32
        )
        grad = scale * lax.dot_general(
            kbuf[:, head(j)], wbuf[j], across_rows, preferred_element_type=jnp.float32
        )
        for r in range(REP):
            cols = pl.ds(pl.multiple_of((j * REP + r) * DH, DH), DH)
            att_ref[:, cols] = mixed[:, r * TOK : (r + 1) * TOK].T.astype(jnp.bfloat16)
            gq_ref[:, cols] = grad[:, r * TOK : (r + 1) * TOK].T.astype(jnp.bfloat16)
        return carry

    lax.fori_loop(0, HK // 2, outputs, 0)
    pass_on(1, 0)
    lax.fori_loop(HK // 2, HK, outputs, 0)
    stores = [
        pltpu.make_async_copy(att_ref, att_out, out_s.at[0]),
        pltpu.make_async_copy(gq_ref, gq_out, out_s.at[1]),
    ]
    for store in stores:
        store.start()
    pass_on(1, 1)

    pass_on(2, 0)
    pass_on(2, 1)
    last = ROWS - 1
    for h, out in ((0, gk_ref), (1, gv_ref)):
        cross(h, last).wait_recv()
        acc[last, h] = acc[last, h] + xrecv[last, h].astype(jnp.float32)

        @pl.when(z < ROWS - 1)
        def _():
            chain_in(h, z).wait_recv()
            acc[last, h] = acc[last, h] + crecv[z, h].astype(jnp.float32)

        @pl.when(z > 0)
        def _():
            chain_in(h, ROWS).wait_recv()
            acc[last, h] = acc[last, h] + crecv[ROWS, h].astype(jnp.float32)

        out[...] = acc[last, h].astype(jnp.bfloat16)

    for store in stores:
        store.wait()
    for h in (0, 1):
        for zz in range(ROWS):
            across(h, zz).wait_send()
            cross(h, zz).wait_send()

    for h in (0, 1):
        for o in range(ROWS - 1):
            chain(h, o).wait_send()
        for k in range(1, ROWS):

            @pl.when((z - (k - 1) >= 0) & (z < ROWS - 1))
            def _():
                along(h, k, True).wait_send()

            @pl.when((z + (k - 1) < ROWS) & (z > 0))
            def _():
                along(h, k, False).wait_send()


def copy_kernel(*refs):
    count = 4
    ins, outs, held = (refs[i * count : (i + 1) * count] for i in range(3))
    sems = refs[3 * count]
    loads = [pltpu.make_async_copy(ins[i], held[i], sems.at[0, i]) for i in range(count)]
    stores = [pltpu.make_async_copy(held[i], outs[i], sems.at[1, i]) for i in range(count)]
    for load in loads:
        load.start()
    for load, store in zip(loads, stores):
        load.wait()
        store.start()
    for store in stores:
        store.wait()


def dense(queries, keys, values, grad_out, positions):
    tokens = TOK * 2 * ROWS
    key_width = HK * DH
    wide = REP * TOK
    bf16, f32 = jnp.bfloat16, jnp.float32
    vmem = pl.BlockSpec(memory_space=pltpu.VMEM)
    dma = pltpu.SemaphoreType.DMA
    anywhere = pl.BlockSpec(memory_space=pl.ANY)
    shapes = [
        jax.ShapeDtypeStruct((TOK, HQ * DH), bf16),
        jax.ShapeDtypeStruct((TOK, HQ * DH), bf16),
        jax.ShapeDtypeStruct((TOK, key_width), bf16),
        jax.ShapeDtypeStruct((TOK, key_width), bf16),
    ]
    results = pl.pallas_call(
        dense_kernel,
        out_shape=shapes,
        in_specs=[vmem] + [anywhere] * 4,
        out_specs=[anywhere] * 2 + [vmem] * 2,
        scratch_shapes=[
            pltpu.VMEM((TOK, HQ * DH), bf16),
            pltpu.VMEM((TOK, HQ * DH), bf16),
            pltpu.VMEM((TOK, HQ * DH), bf16),
            pltpu.VMEM((TOK, HQ * DH), bf16),
            pltpu.VMEM((tokens, key_width), bf16),
            pltpu.VMEM((tokens, key_width), bf16),
            pltpu.VMEM((HK, DH, wide), bf16),
            pltpu.VMEM((HK, DH, wide), bf16),
            pltpu.VMEM((HK, wide, DH), bf16),
            pltpu.VMEM((HK, wide, DH), bf16),
            pltpu.VMEM((HK, tokens, wide), f32),
            pltpu.VMEM((HK, tokens, wide), f32),
            pltpu.VMEM((HK, tokens, wide), bf16),
            pltpu.VMEM((HK, tokens, wide), bf16),
            pltpu.VMEM((HK, 8, wide), f32),
            pltpu.VMEM((HK, 8, wide), f32),
            pltpu.VMEM((HK, 8, wide), f32),
            pltpu.VMEM((ROWS, 2, TOK, key_width), f32),
            pltpu.VMEM((ROWS, 2, TOK, key_width), bf16),
            pltpu.VMEM((ROWS, 2, TOK, key_width), bf16),
            pltpu.VMEM((ROWS - 1, 2, TOK, key_width), bf16),
            pltpu.VMEM((ROWS + 1, 2, TOK, key_width), bf16),
            dma((4,)),
            dma((2,)),
            dma((2, ROWS)),
            dma((2, ROWS)),
            dma((2, ROWS - 1)),
            dma((2, ROWS - 1)),
            dma((2, ROWS - 1)),
            dma((2, ROWS - 1)),
            dma((2, ROWS)),
            dma((2, ROWS)),
            dma((2, ROWS - 1)),
            dma((2, ROWS + 1)),
        ],
        compiler_params=pltpu.CompilerParams(
            collective_id=0, has_side_effects=True, vmem_limit_bytes=56 * 1024 * 1024
        ),
    )(positions.reshape(1, -1), queries, keys, values, grad_out)
    return pl.pallas_call(
        copy_kernel,
        out_shape=shapes,
        in_specs=[anywhere] * 4,
        out_specs=[anywhere] * 4,
        scratch_shapes=[pltpu.VMEM(a.shape, bf16) for a in shapes] + [dma((2, 4))],
    )(*results)


def choose(queries, keys, values, grad_out, positions):
    if lax.axis_size("ctx") == 2 * ROWS and queries.shape[0] == TOK:
        return tuple(dense(queries, keys, values, grad_out, positions))
    return local(queries, keys, values, grad_out, positions)


def solution(mesh):
    in_specs = (
        P(("dp", "ctx"), None),
        P(("dp", "ctx"), None),
        P(("dp", "ctx"), None),
        P(("dp", "ctx"), None),
        P("dp"),
    )
    out_specs = (
        P(("dp", "ctx"), None),
        P(("dp", "ctx"), None),
        P(("dp", "ctx"), None),
        P(("dp", "ctx"), None),
    )
    return jax.shard_map(choose, mesh=mesh, in_specs=in_specs, out_specs=out_specs, check_vma=False)
```
